32 devices in a mesh: dp: 8 (over y, x, core), section: 4 (over z).
Axes of the slice: x: 2, y: 2, z: 4, core: 2. Of those that a mesh axis runs over, the one named last changes fastest.
Arguments:
- inputs: bfloat16 [2, 512, 1024], P(None, 'dp'), may hold values from -6 to 6
- ln_gain: float32 [4, 1024], P('section'), may hold values from 0.5 to 1.5
- w_in: bfloat16 [4, 1024, 2048], P('section'), may hold values from -0.1875 to 0.1875
- w_out: bfloat16 [4, 2048, 1024], P('section'), may hold values from -0.125 to 0.125
- layer_scale: float32 [4, 1024], P('section'), may hold values from 0.25 to 1
- out_grad: bfloat16 [2, 512, 1024], P(None, 'dp'), may hold values from -6 to 6
- owner_table: int32 [8], replicated, may hold values from 0 to 7, each once
Outputs:
- act_factor: float32 [4, 1024, 1024], P('section', 'dp')
- grad_factor: float32 [4, 2048, 2048], P('section', 'dp')
The draws below stay inside these ranges and needn't reach their ends.
Inputs may be any that keep to these rules, and one draw needn't show every extreme that they name: owner_table holds each of 0 .. 7 once.
All inputs are finite; a program needn't handle non-finite values.
Results may differ from the reference program's by a relative error of at most 0.009.
Values may be sent and summed in bfloat16 or wider, within the bound.
No kernel may reach another device: no remote copies, remote signals or barrier semaphores. Data moves between devices by JAX's collectives and lax.ppermute only.
A program may use at most 128 MiB of HBM per device.

```python
import math
import jax
import jax.numpy as jnp
from jax import lax

C = 1024
H = 2048
MB = 2
SECTIONS = 4
TOKENS = 512
N_DP = 8


def block_scale(stream_key, shape, cuts, low, high):
    gain, own = 1.0, jax.random.fold_in(stream_key, 6)
    for position, shards_of in cuts:
        steps = jnp.exp(jax.random.uniform(jax.random.fold_in(own, position), (shards_of,), jnp.float32, low / len(cuts), high / len(cuts)))
        gain = gain * jnp.repeat(steps, shape[position] // shards_of).reshape([-1 if axis == position else 1 for axis in range(len(shape))])
    return gain


def centred(stream_key, extent, scale, most, cuts=(), dtype=jnp.bfloat16):
    array = scale * jax.random.normal(stream_key, extent, jnp.float32)
    if cuts:
        array = array * block_scale(stream_key, extent, cuts, -0.22, 0.18)
    return jnp.clip(array, -most, most).astype(dtype)


def setup_inputs(seed: int = 0) -> dict:
    keys = jax.random.split(jax.random.key(seed), 8)
    inputs = centred(keys[0], (MB, TOKENS, C), 1.0, 6.0, ((1, 8),))
    ln_gain = jnp.clip(1.0 + 0.1 * jax.random.normal(keys[1], (SECTIONS, C), jnp.float32), 0.5, 1.5)
    w_in = centred(keys[2], (SECTIONS, C, H), C ** -0.5, 0.1875, ((0, 4),))
    w_out = centred(keys[3], (SECTIONS, H, C), H ** -0.5, 0.125, ((0, 4),))
    layer_scale = jnp.clip(jnp.exp(math.log(1.0) - 1.3862944 * jax.random.uniform(keys[4], (SECTIONS, C), jnp.float32) ** block_scale(keys[4], (SECTIONS, C), ((0, 4),), -0.2, 0.2)), 0.25, 1.0)
    out_grad = centred(keys[5], (MB, TOKENS, C), 1.0, 6.0, ((1, 8),))
    owner_table = jax.random.permutation(keys[6], N_DP).astype(jnp.int32)
    return {"inputs": inputs, "ln_gain": ln_gain, "w_in": w_in, "w_out": w_out, "layer_scale": layer_scale, "out_grad": out_grad, "owner_table": owner_table}


SQRT_HALF = 0.7071067811865476
INV_ROOT_TAU = 0.3989422804014327

def gelu_exact(values):
    return 0.5 * values * (1.0 + jax.scipy.special.erf(values * SQRT_HALF))

def gelu_slope(values):
    return 0.5 * (1.0 + jax.scipy.special.erf(values * SQRT_HALF)) + values * INV_ROOT_TAU * jnp.exp(-0.5 * values * values)

def normalize(activations, gain_row):
    floats = activations.astype(jnp.float32)
    center = floats - lax.optimization_barrier(jnp.mean(floats, axis=-1, keepdims=True))
    inv_std = lax.rsqrt(lax.optimization_barrier(jnp.mean(center * center, axis=-1, keepdims=True)) + 1e-06)
    normed = center * inv_std
    return ((normed * gain_row).astype(jnp.bfloat16), normed, inv_std)

def forward_block(activations, gain_row, weight_in, weight_out, scales):
    normed_bf, normed, inv_std = normalize(activations, gain_row)
    hidden = jnp.dot(normed_bf, weight_in, preferred_element_type=jnp.float32)
    activated = gelu_exact(hidden).astype(jnp.bfloat16)
    branch = jnp.dot(activated, weight_out, preferred_element_type=jnp.float32)
    output = (activations.astype(jnp.float32) + scales * branch).astype(jnp.bfloat16)
    return (output, normed_bf, normed, inv_std, hidden)

def backward_block(cotangent, normed, inv_std, hidden, gain_row, weight_in, weight_out, scales):
    scaled = (cotangent.astype(jnp.float32) * scales).astype(jnp.bfloat16)
    grad_act = lax.dot_general(scaled, weight_out, (((1,), (1,)), ((), ())), preferred_element_type=jnp.float32)
    grad_hidden = (grad_act * gelu_slope(hidden)).astype(jnp.bfloat16)
    grad_normed = lax.dot_general(grad_hidden, weight_in, (((1,), (1,)), ((), ())), preferred_element_type=jnp.float32) * gain_row
    mean_one = lax.optimization_barrier(jnp.mean(grad_normed, axis=-1, keepdims=True))
    mean_two = lax.optimization_barrier(jnp.mean(grad_normed * normed, axis=-1, keepdims=True))
    grad_input = cotangent.astype(jnp.float32) + inv_std * (grad_normed - mean_one - normed * mean_two)
    return (grad_input.astype(jnp.bfloat16), grad_hidden)

def reorder(square, owner_table):
    owners = owner_table.shape[0]
    blocks = square.reshape(owners, square.shape[0] // owners, square.shape[1])
    return jnp.take(blocks, owner_table, axis=0).reshape(square.shape)

def reference(inputs, ln_gain, w_in, w_out, layer_scale, out_grad, owner_table):
    section_count = ln_gain.shape[0]
    batch_count = inputs.shape[0]
    kept_bf = [[] for section_step in range(section_count)]
    kept_normed = [[] for section_step in range(section_count)]
    kept_inv = [[] for section_step in range(section_count)]
    kept_hidden = [[] for section_step in range(section_count)]
    kept_grads = [[] for section_step in range(section_count)]
    for batch_step in range(batch_count):
        activations = inputs[batch_step]
        for section_step in range(section_count):
            activations, normed_bf, normed, inv_std, hidden = forward_block(activations, ln_gain[section_step], w_in[section_step], w_out[section_step], layer_scale[section_step])
            kept_bf[section_step].append(normed_bf)
            kept_normed[section_step].append(normed)
            kept_inv[section_step].append(inv_std)
            kept_hidden[section_step].append(hidden)
    for batch_step in range(batch_count):
        cotangent = out_grad[batch_step]
        for section_step in reversed(range(section_count)):
            cotangent, grad_hidden = backward_block(cotangent, kept_normed[section_step][batch_step], kept_inv[section_step][batch_step], kept_hidden[section_step][batch_step], ln_gain[section_step], w_in[section_step], w_out[section_step], layer_scale[section_step])
            kept_grads[section_step].append(grad_hidden)
    total_rows = batch_count * inputs.shape[1]
    act_list = []
    grad_list = []
    for section_step in range(section_count):
        act_rows = jnp.concatenate(kept_bf[section_step], axis=0)
        grad_rows = jnp.concatenate(kept_grads[section_step], axis=0)
        act_square = jnp.dot(act_rows.T, act_rows, preferred_element_type=jnp.float32) / total_rows
        grad_square = jnp.dot(grad_rows.T, grad_rows, preferred_element_type=jnp.float32) / total_rows
        act_list.append(reorder(act_square, owner_table))
        grad_list.append(reorder(grad_square, owner_table))
    return (jnp.stack(act_list), jnp.stack(grad_list))
```

```python
import jax
import jax.numpy as jnp
from jax import lax
from jax.sharding import PartitionSpec as P

SQRT_HALF = 0.7071067811865476
INV_ROOT_TAU = 0.3989422804014327


def hop(value, source, steps):
    return lax.ppermute(value, "section", [(source, source + steps)])


def swapped(value, axis, mask):
    count = lax.axis_size(axis)
    return lax.ppermute(value, axis, [(source, source ^ mask) for source in range(count)])


def turned(value, axis, steps):
    count = lax.axis_size(axis)
    return lax.ppermute(value, axis, [(source, (source + steps) % count) for source in range(count)])


def gathered(value, axis):
    count = lax.axis_size(axis)
    if count & (count - 1):
        return [value] + [turned(value, axis, steps) for steps in range(1, count)]
    if count == 1:
        return [value]
    blocks = [value] + [swapped(value, axis, mask) for mask in range(2, count, 2)]
    return blocks + [swapped(block, axis, 1) for block in blocks]


def gelu_exact(values):
    return 0.5 * values * (1.0 + jax.scipy.special.erf(values * SQRT_HALF))


def gelu_slope(values):
    return 0.5 * (
        1.0 + jax.scipy.special.erf(values * SQRT_HALF)
    ) + values * INV_ROOT_TAU * jnp.exp(-0.5 * values * values)


def normalize(activations, gain_row):
    floats = activations.astype(jnp.float32)
    center = floats - jnp.mean(floats, axis=-1, keepdims=True)
    inv_std = lax.rsqrt(jnp.mean(center * center, axis=-1, keepdims=True) + 1e-06)
    normed = center * inv_std
    return ((normed * gain_row).astype(jnp.bfloat16), normed, inv_std)


def forward_block(activations, gain_row, weight_in, weight_out, scales):
    normed_bf, _, _ = normalize(activations, gain_row)
    hidden = jnp.dot(normed_bf, weight_in, preferred_element_type=jnp.float32)
    activated = gelu_exact(hidden).astype(jnp.bfloat16)
    branch = jnp.dot(activated, weight_out, preferred_element_type=jnp.float32)
    return (activations.astype(jnp.float32) + scales * branch).astype(jnp.bfloat16)


def hidden_grad(cotangent, slope, weight_out, scales):
    scaled = (cotangent.astype(jnp.float32) * scales).astype(jnp.bfloat16)
    grad_act = lax.dot_general(
        scaled, weight_out, (((1,), (1,)), ((), ())), preferred_element_type=jnp.float32
    )
    return (grad_act * slope).astype(jnp.bfloat16)


def input_grad(cotangent, grad_hidden, normed, inv_std, gain_row, weight_in):
    grad_normed = (
        lax.dot_general(
            grad_hidden, weight_in, (((1,), (1,)), ((), ())), preferred_element_type=jnp.float32
        )
        * gain_row
    )
    mean_one = jnp.mean(grad_normed, axis=-1, keepdims=True)
    mean_two = jnp.mean(grad_normed * normed, axis=-1, keepdims=True)
    grad_input = cotangent.astype(jnp.float32) + inv_std * (
        grad_normed - mean_one - normed * mean_two
    )
    return grad_input.astype(jnp.bfloat16)


def owned_square(blocks, owner, owners, total_rows):
    rows = jnp.concatenate(blocks, axis=0)
    width = rows.shape[1] // owners
    own = lax.dynamic_slice_in_dim(rows, owner * width, width, axis=1)
    product = lax.dot_general(
        own, rows, (((0,), (0,)), ((), ())), preferred_element_type=jnp.float32
    )
    return product / total_rows


def body(inputs, ln_gain, w_in, w_out, layer_scale, out_grad, owner_table):
    gain_row = ln_gain[0]
    weight_in = w_in[0]
    weight_out = w_out[0]
    scales = layer_scale[0]
    section_count = lax.axis_size("section")
    dp_count = lax.axis_size("dp")
    section_index = lax.axis_index("section")
    batch_count, row_count, _ = inputs.shape
    total_rows = batch_count * row_count * dp_count
    owner = owner_table[lax.axis_index("dp")]
    batches = range(batch_count)

    held = [inputs[m] for m in batches]
    for step in range(section_count - 1):
        for m in batches:
            output = forward_block(held[m], gain_row, weight_in, weight_out, scales)
            arrived = hop(output, step, 1)
            held[m] = jnp.where(section_index == step + 1, arrived, held[m])
    saved = []
    for m in batches:
        normed_bf, normed, inv_std = normalize(held[m], gain_row)
        hidden = jnp.dot(normed_bf, weight_in, preferred_element_type=jnp.float32)
        saved.append((normed_bf, normed, inv_std, gelu_slope(hidden)))

    returning = [out_grad[m] for m in batches]
    for step in range(section_count - 1, 0, -1):
        for m in batches:
            _, normed, inv_std, slope = saved[m]
            grad_hidden = hidden_grad(returning[m], slope, weight_out, scales)
            grad_input = input_grad(
                returning[m], grad_hidden, normed, inv_std, gain_row, weight_in
            )
            arrived = hop(grad_input, step, -1)
            returning[m] = jnp.where(section_index == step - 1, arrived, returning[m])
    act_blocks, grad_blocks = [], []
    for m in batches:
        act_blocks += gathered(saved[m][0], "dp")
    for m in batches:
        grad_blocks += gathered(hidden_grad(returning[m], saved[m][3], weight_out, scales), "dp")
    act_share = owned_square(act_blocks, owner, dp_count, total_rows)
    grad_share = owned_square(grad_blocks, owner, dp_count, total_rows)
    return (act_share[None], grad_share[None])


def solution(mesh):
    placed = (
        P(None, "dp", None),
        P("section", None),
        P("section", None, None),
        P("section", None, None),
        P("section", None),
        P(None, "dp", None),
        P(),
    )
    return jax.shard_map(
        body,
        mesh=mesh,
        in_specs=placed,
        out_specs=(P("section", "dp", None), P("section", "dp", None)),
        check_vma=False,
    )
```

```python
import functools

import jax
import jax.numpy as jnp
from jax import lax
from jax.experimental import pallas as pl
from jax.experimental.pallas import tpu as pltpu
from jax.sharding import PartitionSpec as P

SQRT_HALF = 0.7071067811865476
INV_ROOT_TAU = 0.3989422804014327
F32 = jnp.float32
BF16 = jnp.bfloat16
IN_VMEM = pl.BlockSpec(memory_space=pltpu.VMEM)
IN_SMEM = pl.BlockSpec(memory_space=pltpu.SMEM)
TILE = 512
MIB = 2**20


def hop(value, source, steps):
    return lax.ppermute(value, "section", [(source, source + steps)])


def swapped(value, axis, mask):
    count = lax.axis_size(axis)
    return lax.ppermute(value, axis, [(source, source ^ mask) for source in range(count)])


def turned(value, axis, steps):
    count = lax.axis_size(axis)
    return lax.ppermute(value, axis, [(source, (source + steps) % count) for source in range(count)])


def gathered(value, axis):
    count = lax.axis_size(axis)
    if count & (count - 1):
        return [value] + [turned(value, axis, steps) for steps in range(1, count)]
    if count == 1:
        return [value]
    blocks = [value] + [swapped(value, axis, mask) for mask in range(2, count, 2)]
    return blocks + [swapped(block, axis, 1) for block in blocks]


def tiles(width):
    size = min(TILE, width)
    return [slice(start, min(start + size, width)) for start in range(0, width, size)]


def dot_nt(left, right):
    return lax.dot_general(left, right, (((1,), (1,)), ((), ())), preferred_element_type=F32)


def dot_tn(left, right):
    return lax.dot_general(left, right, (((0,), (0,)), ((), ())), preferred_element_type=F32)


def normalize(floats, gain_row):
    center = floats - jnp.mean(floats, axis=-1, keepdims=True)
    inv_std = lax.rsqrt(jnp.mean(center * center, axis=-1, keepdims=True) + 1e-06)
    normed = center * inv_std
    return ((normed * gain_row).astype(BF16), normed, inv_std)


def forward_kernel(here, x_ref, gain, weight_in, weight_out, scales, out, acted):
    @pl.when(here[0] == 1)
    def _():
        x = x_ref[...].astype(F32)
        normed_bf, _, _ = normalize(x, gain[...])
        for cols in tiles(weight_in.shape[1]):
            hidden = jnp.dot(normed_bf, weight_in[:, cols], preferred_element_type=F32)
            acted[:, cols] = (0.5 * hidden * (1.0 + lax.erf(hidden * SQRT_HALF))).astype(BF16)
        for cols in tiles(x.shape[1]):
            branch = jnp.dot(acted[...], weight_out[:, cols], preferred_element_type=F32)
            out[:, cols] = (x[:, cols] + scales[:, cols] * branch).astype(BF16)


def save_kernel(count, where, *refs):
    held, (gain, weight_in, normed_bf, normed, inv_std, slope, chosen) = refs[:count], refs[count:]
    for index, ref in enumerate(held):
        @pl.when(where[0] == index)
        def _():
            chosen[...] = ref[...]

    normed_bf[...], normed[...], inv_std[...] = normalize(chosen[...].astype(F32), gain[...])
    for cols in tiles(weight_in.shape[1]):
        v = jnp.dot(normed_bf[...], weight_in[:, cols], preferred_element_type=F32)
        slope[:, cols] = 0.5 * (1.0 + lax.erf(v * SQRT_HALF)) + v * INV_ROOT_TAU * jnp.exp(
            -0.5 * v * v
        )


def hidden_grad(cotangent, scales, weight_out, slope, grad_hidden):
    scaled = (cotangent * scales).astype(BF16)
    for cols in tiles(weight_out.shape[0]):
        grad_act = dot_nt(scaled, weight_out[cols, :])
        grad_hidden[:, cols] = (grad_act * slope[:, cols]).astype(BF16)


def backward_kernel(
    here, gy_ref, gain, weight_in, weight_out, scales, normed_ref, inv_std, slope, out, grad_hidden
):
    @pl.when(here[0] == 1)
    def _():
        cotangent = gy_ref[...].astype(F32)
        hidden_grad(cotangent, scales[...], weight_out, slope, grad_hidden)
        grad_normed = dot_nt(grad_hidden[...], weight_in[...]) * gain[...]
        normed = normed_ref[...]
        mean_one = jnp.mean(grad_normed, axis=-1, keepdims=True)
        mean_two = jnp.mean(grad_normed * normed, axis=-1, keepdims=True)
        out[...] = (
            cotangent + inv_std[...] * (grad_normed - mean_one - normed * mean_two)
        ).astype(BF16)


def last_kernel(count, where, *refs):
    held, (scales, weight_out, slope, grad_hidden, chosen) = refs[:count], refs[count:]
    for index, ref in enumerate(held):
        @pl.when(where[0] == index)
        def _():
            chosen[...] = ref[...]

    hidden_grad(chosen[...].astype(F32), scales[...], weight_out, slope, grad_hidden)


def square_kernel(count, factor, owner, *refs):
    blocks, (total, rows) = refs[:count], refs[count:]
    height = blocks[0].shape[0]

    @pl.when(pl.program_id(0) == 0)
    def _():
        for index, ref in enumerate(blocks):
            rows[index * height : (index + 1) * height, :] = ref[...]

    wide, tall = total.shape[1], total.shape[0]
    own = rows[:, pl.ds(pl.multiple_of(owner[0] * tall, tall), tall)]
    here = rows[:, pl.ds(pl.multiple_of(pl.program_id(0) * wide, wide), wide)]
    total[...] = dot_tn(own, here) * factor


def pinned(value):
    return pltpu.with_memory_space_constraint(value, pltpu.VMEM)


def call(kernel, scalars, arrays, outs, scratch=(), flops=0, room=24 * MIB):
    moved = sum(array.size * array.dtype.itemsize for array in arrays)
    return pl.pallas_call(
        kernel,
        in_specs=[IN_SMEM] * len(scalars) + [IN_VMEM] * len(arrays),
        out_specs=[IN_VMEM] * len(outs),
        out_shape=outs,
        scratch_shapes=list(scratch),
        compiler_params=pltpu.CompilerParams(vmem_limit_bytes=room),
        cost_estimate=pl.CostEstimate(flops=flops, bytes_accessed=moved, transcendentals=0),
    )(*scalars, *arrays)


def owned_square(blocks, owner, owners, total_rows):
    height, width = blocks[0].shape
    tall = width // owners
    wide = min(TILE, width)
    if tall % 128 or width % wide:
        rows = jnp.concatenate(blocks, axis=0)
        own = lax.dynamic_slice_in_dim(rows, owner[0] * tall, tall, axis=1)
        return dot_tn(own, rows) / total_rows
    count = len(blocks)
    depth = height * count
    return pl.pallas_call(
        functools.partial(square_kernel, count, 1.0 / total_rows),
        grid=(width // wide,),
        in_specs=[IN_SMEM] + [pl.BlockSpec((height, width), lambda step: (0, 0))] * count,
        out_specs=pl.BlockSpec((tall, wide), lambda step: (0, step)),
        out_shape=jax.ShapeDtypeStruct((tall, width), F32),
        scratch_shapes=[pltpu.VMEM((depth, width), BF16)],
        compiler_params=pltpu.CompilerParams(vmem_limit_bytes=40 * MIB),
        cost_estimate=pl.CostEstimate(
            flops=2 * depth * tall * width, bytes_accessed=2 * depth * width, transcendentals=0
        ),
    )(owner, *blocks)


def body(inputs, ln_gain, w_in, w_out, layer_scale, out_grad, owner_table):
    weight_in = pinned(w_in[0])
    weight_out = pinned(w_out[0])
    section_count = lax.axis_size("section")
    dp_count = lax.axis_size("dp")
    section_index = lax.axis_index("section")
    batch_count, row_count, width = inputs.shape
    width_hidden = w_in.shape[2]
    total_rows = batch_count * row_count * dp_count
    owner = owner_table[lax.axis_index("dp")].reshape(1)
    where = section_index.reshape(1)
    batches = range(batch_count)
    product = 2 * row_count * width * width_hidden
    block = jax.ShapeDtypeStruct((row_count, width), BF16)
    wide_scratch = pltpu.VMEM((row_count, width_hidden), BF16)

    def active(step):
        return (section_index == step).astype(jnp.int32).reshape(1)

    held = [[inputs[m]] for m in batches]
    for step in range(section_count - 1):
        for m in batches:
            (output,) = call(
                forward_kernel,
                [active(step)],
                [held[m][-1], ln_gain, weight_in, weight_out, layer_scale],
                [block],
                [wide_scratch],
                2 * product,
            )
            held[m].append(hop(output, step, 1))

    saved = [None] * batch_count
    returned = [[out_grad[m]] for m in batches]
    for step in range(section_count - 1, 0, -1):
        for m in batches:
            if saved[m] is None:
                saved[m] = call(
                    functools.partial(save_kernel, section_count),
                    [where],
                    [*held[m], ln_gain, weight_in],
                    [
                        block,
                        jax.ShapeDtypeStruct((row_count, width), F32),
                        jax.ShapeDtypeStruct((row_count, 1), F32),
                        jax.ShapeDtypeStruct((row_count, width_hidden), F32),
                    ],
                    [pltpu.VMEM((row_count, width), BF16)],
                    product,
                )
            _, normed, inv_std, slope = saved[m]
            (grad_input,) = call(
                backward_kernel,
                [active(step)],
                [
                    returned[m][0], ln_gain, weight_in, weight_out, layer_scale,
                    pinned(normed), pinned(inv_std), pinned(slope),
                ],
                [block],
                [wide_scratch],
                2 * product,
            )
            returned[m].insert(0, hop(grad_input, step, -1))

    act_blocks, grad_blocks = [], []
    for m in batches:
        act_blocks += gathered(saved[m][0], "dp")
    for m in batches:
        (grad_hidden,) = call(
            functools.partial(last_kernel, section_count),
            [where],
            [*returned[m], layer_scale, weight_out, pinned(saved[m][3])],
            [jax.ShapeDtypeStruct((row_count, width_hidden), BF16)],
            [pltpu.VMEM((row_count, width), BF16)],
            product,
        )
        grad_blocks += gathered(grad_hidden, "dp")
    act_share = owned_square(act_blocks, owner, dp_count, total_rows)
    grad_share = owned_square(grad_blocks, owner, dp_count, total_rows)
    return (act_share[None], grad_share[None])


def solution(mesh):
    placed = (
        P(None, "dp", None),
        P("section", None),
        P("section", None, None),
        P("section", None, None),
        P("section", None),
        P(None, "dp", None),
        P(),
    )
    return jax.shard_map(
        body,
        mesh=mesh,
        in_specs=placed,
        out_specs=(P("section", "dp", None), P("section", "dp", None)),
        check_vma=False,
    )
```

```python
import functools

import jax
import jax.numpy as jnp
from jax import lax
from jax.experimental import pallas as pl
from jax.experimental.pallas import tpu as pltpu
from jax.sharding import PartitionSpec as P

SQRT_HALF = 0.7071067811865476
INV_ROOT_TAU = 0.3989422804014327
F32 = jnp.float32
BF16 = jnp.bfloat16
IN_VMEM = pl.BlockSpec(memory_space=pltpu.VMEM)
IN_SMEM = pl.BlockSpec(memory_space=pltpu.SMEM)
ANYWHERE = pl.BlockSpec(memory_space=pl.ANY)
TILE = 512
MIB = 2**20
ROOM = 24 * MIB


def hop(value, source, steps):
    return lax.ppermute(value, "section", [(source, source + steps)])


def swapped(value, axis, mask):
    count = lax.axis_size(axis)
    return lax.ppermute(value, axis, [(source, source ^ mask) for source in range(count)])


def tiles(width, most=TILE):
    size = min(most, width)
    return [slice(start, min(start + size, width)) for start in range(0, width, size)]


def dot(left, right):
    return jnp.dot(left, right, preferred_element_type=F32)


def dot_tn(left, right):
    return lax.dot_general(left, right, (((0,), (0,)), ((), ())), preferred_element_type=F32)


def normalize(floats, gain_row):
    center = floats - jnp.mean(floats, axis=-1, keepdims=True)
    inv_std = lax.rsqrt(jnp.mean(center * center, axis=-1, keepdims=True) + 1e-06)
    normed = center * inv_std
    return ((normed * gain_row).astype(BF16), normed, inv_std)


def gelu(v):
    return 0.5 * v * (1.0 + lax.erf(v * SQRT_HALF))


def gelu_slope(v):
    return 0.5 * (1.0 + lax.erf(v * SQRT_HALF)) + v * INV_ROOT_TAU * jnp.exp(-0.5 * v * v)


def first_kernel(*refs):
    far, near, (out, acted, arrived) = refs[:6], refs[6:12], refs[12:]
    gain, x_all, weight_in, weight_out, scales, _ = near
    in_tiles, out_tiles = tiles(weight_in.shape[1]), tiles(weight_out.shape[0])
    pairs = [(far[0], gain), (far[1], x_all)]
    pairs += [(far[2].at[0, :, cols], weight_in.at[:, cols]) for cols in in_tiles]
    pairs += [(far[3].at[0, rows, :], weight_out.at[rows, :]) for rows in out_tiles]
    pairs += [(far[4], scales), (far[5], near[5])]
    copies = [
        pltpu.make_async_copy(source, target, arrived.at[index])
        for index, (source, target) in enumerate(pairs)
    ]
    for copy in copies:
        copy.start()
    mine = lax.axis_index("section") == 0
    copies[0].wait()
    copies[1].wait()
    x = x_all[0].astype(F32)
    normed_bf, _, _ = normalize(x, gain[...])
    for copy, cols in zip(copies[2:], in_tiles):
        copy.wait()

        @pl.when(mine)
        def _():
            acted[:, cols] = gelu(dot(normed_bf, weight_in[:, cols])).astype(BF16)

    for copy in copies[2 + len(in_tiles) :]:
        copy.wait()

    @pl.when(mine)
    def _():
        for cols in tiles(x.shape[1]):
            branch = dot(acted[...], weight_out[:, cols])
            out[:, cols] = (x[:, cols] + scales[:, cols] * branch).astype(BF16)


def turn_kernel(weight_in, weight_out, turned_in, turned_out):
    for ref, turned in ((weight_in, turned_in), (weight_out, turned_out)):
        for rows in tiles(ref.shape[0]):
            for cols in tiles(ref.shape[1]):
                turned[cols, rows] = ref[rows, cols].T


def forward_kernel(step, batch, x_ref, gain, weight_in, weight_out, scales, *refs):
    out, acted = refs[-2:]
    @pl.when(lax.axis_index("section") == step)
    def _():
        x = (x_ref[...] if batch is None else x_ref[batch]).astype(F32)
        normed_bf, _, _ = normalize(x, gain[...])
        for cols in tiles(weight_in.shape[1]):
            acted[:, cols] = gelu(dot(normed_bf, weight_in[:, cols])).astype(BF16)
        for cols in tiles(x.shape[1]):
            branch = dot(acted[...], weight_out[:, cols])
            out[:, cols] = (x[:, cols] + scales[:, cols] * branch).astype(BF16)


def choose(whole, batch, place, later, chosen):
    section = lax.axis_index("section")

    @pl.when(section == place)
    def _():
        chosen[...] = whole[batch]

    for index, ref in later:
        @pl.when(section == index)
        def _():
            chosen[...] = ref[...]


def save_kernel(batch, sections, *refs):
    whole, later, refs = refs[0], refs[1:sections], refs[sections:]
    gain, weight_in, normed_bf, normed, inv_std, slope, chosen = refs
    choose(whole, batch, 0, list(enumerate(later, 1)), chosen)
    normed_bf[...], normed[...], inv_std[...] = normalize(chosen[...].astype(F32), gain[...])
    for cols in tiles(weight_in.shape[1]):
        slope[:, cols] = gelu_slope(dot(normed_bf[...], weight_in[:, cols]))


def backward_kernel(
    step, batch, merged, gy_ref, gain, turned_in, turned_out, scales, normed_ref, inv_std, slope, *refs
):
    parts, out, grad_hidden = refs[:merged], refs[-2], refs[-1]
    if merged:
        out, whole = refs[merged], refs[merged + 1]
        height = whole.shape[0] // merged
        for index, part in enumerate(parts):
            whole[index * height : (index + 1) * height, :] = part[...]

    @pl.when(lax.axis_index("section") == step)
    def _():
        cotangent = (gy_ref[...] if batch is None else gy_ref[batch]).astype(F32)
        scaled = (cotangent * scales[...]).astype(BF16)
        for cols in tiles(turned_out.shape[1]):
            grad_act = dot(scaled, turned_out[:, cols])
            grad_hidden[:, cols] = (grad_act * slope[:, cols]).astype(BF16)
        grad_normed = dot(grad_hidden[...], turned_in[...]) * gain[...]
        normed = normed_ref[...]
        mean_one = jnp.mean(grad_normed, axis=-1, keepdims=True)
        mean_two = jnp.mean(grad_normed * normed, axis=-1, keepdims=True)
        out[...] = (
            cotangent + inv_std[...] * (grad_normed - mean_one - normed * mean_two)
        ).astype(BF16)


def pick_kernel(batch, sections, *refs):
    whole, later, chosen = refs[0], refs[1:sections], refs[-1]
    choose(whole, batch, sections - 1, list(enumerate(later)), chosen)


def slopes_kernel(count, batches, *refs):
    blocks, (weight_in, _, rows), slopes = refs[:count], refs[count : count + 3], refs[count + 3 :]
    height = blocks[0].shape[0]
    part = height // batches
    for batch in range(batches):
        for index, block in enumerate(blocks):
            start = (batch * count + index) * part
            rows[start : start + part, :] = block[batch * part : (batch + 1) * part, :]
    for batch, slope in enumerate(slopes):
        size = count * part
        for high in tiles(size, 256):
            mine = rows[batch * size + high.start : batch * size + high.stop, :]
            for cols in tiles(weight_in.shape[1], 256):
                slope[high, cols] = gelu_slope(dot(mine, weight_in[:, cols]))


def hidden_kernel(count, *refs):
    blocks, (scales, turned_out, slope, grad_hidden, scaled) = refs[:count], refs[count:]
    part = blocks[0].shape[0]
    for index, block in enumerate(blocks):
        scaled[index * part : (index + 1) * part, :] = (
            block[...].astype(F32) * scales[...]
        ).astype(BF16)
    for cols in tiles(turned_out.shape[1], 256):
        grad_act = dot(scaled[...], turned_out[:, cols])
        grad_hidden[:, cols] = (grad_act * slope[:, cols]).astype(BF16)


def square_kernel(count, factor, summed, owner_table, *refs):
    blocks, earlier, (total, stage, left) = refs[:count], refs[count:-3], refs[-3:]
    tall, width = stage.shape
    mine = pl.ds(pl.multiple_of(owner_table[lax.axis_index("dp")] * tall, tall), tall)
    pieces = tiles(width)
    copies = [
        pltpu.make_async_copy(stage.at[:, cols], total.at[:, cols], left.at[index])
        for index, cols in enumerate(pieces)
    ]
    own = [block[:, mine].T for block in blocks]
    for copy, cols in zip(copies, pieces):
        value = earlier[0][:, cols] if summed else None
        for mine_turned, block in zip(own, blocks):
            term = dot(mine_turned, block[:, cols])
            value = term if value is None else value + term
        stage[:, cols] = value * factor
        copy.start()
    for copy in copies:
        copy.wait()


def partial_kernel(count, owner_table, *refs):
    blocks, total = refs[:count], refs[-1]
    tall = total.shape[0]
    mine = pl.ds(pl.multiple_of(owner_table[lax.axis_index("dp")] * tall, tall), tall)
    own = [block[:, mine].T for block in blocks]
    for cols in tiles(total.shape[1]):
        value = None
        for mine_turned, block in zip(own, blocks):
            term = dot(mine_turned, block[:, cols])
            value = term if value is None else value + term
        total[:, cols] = value


def pinned(value):
    return pltpu.with_memory_space_constraint(value, pltpu.VMEM)


def shape(dims, dtype=BF16):
    return jax.ShapeDtypeStruct(dims, dtype)


def call(kernel, arrays, outs, scratch=(), flops=0, specs=None, name=None):
    return pl.pallas_call(
        kernel,
        in_specs=specs or [IN_VMEM] * len(arrays),
        out_specs=[IN_VMEM] * len(outs),
        out_shape=outs,
        scratch_shapes=list(scratch),
        compiler_params=pltpu.CompilerParams(vmem_limit_bytes=ROOM),
        cost_estimate=pl.CostEstimate(flops=flops, bytes_accessed=8 * MIB, transcendentals=0),
        name=name,
    )(*arrays)


def owned_square(blocks, owner_table, owners, factor, earlier=None, extra=()):
    width = blocks[0].shape[1]
    tall = width // owners
    depth = sum(block.shape[0] for block in blocks)
    before = [] if earlier is None else [pinned(earlier)]
    count = len(blocks)
    flops = 2 * depth * tall * width
    specs = [IN_SMEM] + [IN_VMEM] * (count + len(before)) + [ANYWHERE] * len(extra)
    arrays = [owner_table, *[pinned(block) for block in blocks], *before, *extra]
    if factor is None:
        return call(
            functools.partial(partial_kernel, count),
            arrays,
            [shape((tall, width), F32)],
            flops=flops,
            specs=specs,
            name="partial",
        )[0]
    return pl.pallas_call(
        functools.partial(square_kernel, count, factor, bool(before)),
        in_specs=specs,
        out_specs=pl.BlockSpec(memory_space=pltpu.HBM),
        out_shape=shape((tall, width), F32),
        scratch_shapes=[
            pltpu.VMEM((tall, width), F32),
            pltpu.SemaphoreType.DMA((len(tiles(width)),)),
        ],
        compiler_params=pltpu.CompilerParams(vmem_limit_bytes=ROOM),
        cost_estimate=pl.CostEstimate(
            flops=flops, bytes_accessed=4 * tall * width, transcendentals=0
        ),
        name="square",
    )(*arrays)


def plain_square(rows, owner_table, owners, total_rows):
    everything = lax.all_gather(rows, "dp", axis=0, tiled=True)
    tall = rows.shape[1] // owners
    start = owner_table[lax.axis_index("dp")] * tall
    own = lax.dynamic_slice_in_dim(everything, start, tall, axis=1)
    return dot_tn(own, everything) / total_rows


def body(inputs, ln_gain, w_in, w_out, layer_scale, out_grad, owner_table):
    sections = lax.axis_size("section")
    owners = lax.axis_size("dp")
    batch_count, row_count, width = inputs.shape
    width_hidden = w_in.shape[2]
    total_rows = batch_count * row_count * owners
    batches = range(batch_count)
    product = 2 * row_count * width * width_hidden
    block = shape((row_count, width))
    wide = pltpu.VMEM((row_count, width_hidden), BF16)
    flat = pltpu.VMEM((row_count, width), BF16)
    far = [ln_gain, inputs, w_in, w_out, layer_scale, out_grad]
    sizes = [ln_gain.shape, inputs.shape, w_in.shape[1:], w_out.shape[1:], ln_gain.shape, inputs.shape]
    *near, output = call(
        first_kernel,
        [pltpu.with_memory_space_constraint(value, pltpu.HBM) for value in far],
        [pltpu.VMEM(size, value.dtype) for size, value in zip(sizes, far)] + [block],
        [wide, pltpu.SemaphoreType.DMA((4 + 2 * len(tiles(width_hidden)),))],
        2 * product,
        [pl.BlockSpec(memory_space=pltpu.HBM)] * len(far),
        "first",
    )
    paired = owners in (2, 4, 8) and not (width // owners % 128 or width_hidden // owners % 128)
    masks = range(2, owners, 2)
    gain, given, weight_in, weight_out, scales, asked = [pinned(value) for value in near]
    arrived, after = [[] for m in batches], []
    for step in range(sections - 1):
        for m in batches:
            if step or m:
                (output,) = call(
                    functools.partial(forward_kernel, step, None if step else m),
                    [arrived[m][-1] if step else given, gain, weight_in, weight_out, scales, *after],
                    [block],
                    [wide],
                    2 * product,
                    [IN_VMEM] * 5 + [ANYWHERE] * len(after),
                    "forward",
                )
            arrived[m].append(pinned(hop(output, step, 1)))
        if step == 0:
            turned_in, turned_out = call(
                turn_kernel,
                [weight_in, weight_out],
                [pltpu.VMEM((width_hidden, width), BF16), pltpu.VMEM((width, width_hidden), BF16)],
                name="turn",
            )
            turned_in, turned_out = pinned(turned_in), pinned(turned_out)
            after = [turned_in]

    saved, returned, gathered = [], [[] for m in batches], None
    for step in range(sections - 1, 0, -1):
        for m in batches:
            if len(saved) <= m:
                values = call(
                    functools.partial(save_kernel, m, sections),
                    [given, *arrived[m], gain, weight_in],
                    [
                        block,
                        shape((row_count, width), F32),
                        shape((row_count, 1), F32),
                        shape((row_count, width_hidden), F32),
                    ],
                    [flat],
                    product,
                    name="save",
                )
                saved.append([pinned(value) for value in values])
            merge = [saved[n][0] for n in batches] if step == sections - 1 and m == batches[-1] else []
            outs = [block] + ([shape((batch_count * row_count, width))] if merge else [])
            grad_input, *rest = call(
                functools.partial(
                    backward_kernel, step, m if step == sections - 1 else None, len(merge)
                ),
                [
                    asked if step == sections - 1 else returned[m][0],
                    gain, turned_in, turned_out, scales, *saved[m][1:], *merge,
                ],
                outs,
                [wide],
                2 * product,
                name="backward",
            )
            returned[m].insert(0, pinned(hop(grad_input, step, -1)))
        if rest:
            merged = rest[0]
        if rest and paired:
            gathered = [merged] + [swapped(merged, "dp", mask) for mask in masks]
        if paired and step == max(sections - 2, 1):
            count = len(gathered)
            rows, *slopes = call(
                functools.partial(slopes_kernel, count, batch_count),
                [*[pinned(x) for x in gathered], weight_in, grad_input],
                [shape((count * batch_count * row_count, width))]
                + [shape((count * row_count, width_hidden), F32)] * batch_count,
                flops=product * count * batch_count,
                specs=[IN_VMEM] * (count + 1) + [ANYWHERE],
                name="slopes",
            )
            act_blocks = [rows, swapped(rows, "dp", 1)]

    cotangents = [
        call(
            functools.partial(pick_kernel, m, sections),
            [asked, *returned[m], *([pinned(slopes[m])] if paired else [])],
            [block],
            specs=[IN_VMEM] * sections + [ANYWHERE] * paired,
            name="pick",
        )[0]
        for m in batches
    ]
    hidden_blocks = []
    for m in batches:
        near = [cotangents[m]] + [swapped(cotangents[m], "dp", mask) for mask in masks if paired]
        count = len(near)
        (grad_hidden,) = call(
            functools.partial(hidden_kernel, count),
            [*[pinned(x) for x in near], scales, turned_out, pinned(slopes[m]) if paired else saved[m][3]],
            [shape((count * row_count, width_hidden))],
            [pltpu.VMEM((count * row_count, width), BF16)],
            product * count,
            name="hidden",
        )
        hidden_blocks += [grad_hidden] + ([swapped(grad_hidden, "dp", 1)] if paired else [])
    if not paired:
        grad_rows = jnp.concatenate(hidden_blocks, axis=0)
        return (
            plain_square(merged, owner_table, owners, total_rows)[None],
            plain_square(grad_rows, owner_table, owners, total_rows)[None],
        )
    factor = 1.0 / total_rows
    act_share = owned_square(act_blocks, owner_table, owners, factor, extra=hidden_blocks[:1])
    earlier = owned_square(hidden_blocks[:-1], owner_table, owners, None)
    grad_share = owned_square(hidden_blocks[-1:], owner_table, owners, factor, earlier)
    return (act_share[None], grad_share[None])


def solution(mesh):
    placed = (
        P(None, "dp", None),
        P("section", None),
        P("section", None, None),
        P("section", None, None),
        P("section", None),
        P(None, "dp", None),
        P(),
    )
    return jax.shard_map(
        body,
        mesh=mesh,
        in_specs=placed,
        out_specs=(P("section", "dp", None), P("section", "dp", None)),
        check_vma=False,
    )
```

```python
import functools

import jax
import jax.numpy as jnp
from jax import lax
from jax.experimental import pallas as pl
from jax.experimental.pallas import tpu as pltpu
from jax.sharding import PartitionSpec as P

SQRT_HALF = 0.7071067811865476
INV_ROOT_TAU = 0.3989422804014327
F32 = jnp.float32
BF16 = jnp.bfloat16
IN_VMEM = pl.BlockSpec(memory_space=pltpu.VMEM)
IN_SMEM = pl.BlockSpec(memory_space=pltpu.SMEM)
TILE = 512
MIB = 2**20
ROOM = 24 * MIB


def hop(value, source, steps):
    return lax.ppermute(value, "section", [(source, source + steps)])


def swapped(value, axis, mask):
    count = lax.axis_size(axis)
    return lax.ppermute(value, axis, [(source, source ^ mask) for source in range(count)])


def tiles(width, most=TILE):
    size = min(most, width)
    return [slice(start, min(start + size, width)) for start in range(0, width, size)]


def dot(left, right):
    return jnp.dot(left, right, preferred_element_type=F32)


def dot_tn(left, right):
    return lax.dot_general(left, right, (((0,), (0,)), ((), ())), preferred_element_type=F32)


def normalize(floats, gain_row):
    center = floats - jnp.mean(floats, axis=-1, keepdims=True)
    inv_std = lax.rsqrt(jnp.mean(center * center, axis=-1, keepdims=True) + 1e-06)
    normed = center * inv_std
    return ((normed * gain_row).astype(BF16), normed, inv_std)


def gelu(v):
    return 0.5 * v * (1.0 + lax.erf(v * SQRT_HALF))


def gelu_slope(v):
    return 0.5 * (1.0 + lax.erf(v * SQRT_HALF)) + v * INV_ROOT_TAU * jnp.exp(-0.5 * v * v)


def arrivals(far, near, arrived):
    gain, x_all, weight_in, weight_out, scales, asked = near
    pairs = [(far[0], gain), (far[1], x_all)]
    pairs += [(far[2].at[0, :, cols], weight_in.at[:, cols]) for cols in tiles(weight_in.shape[1])]
    pairs += [(far[3].at[0, rows, :], weight_out.at[rows, :]) for rows in tiles(weight_out.shape[0])]
    pairs += [(far[4], scales), (far[5], asked)]
    return [
        pltpu.make_async_copy(source, target, arrived.at[index])
        for index, (source, target) in enumerate(pairs)
    ]


def first_kernel(*refs):
    far, near, (out, acted, arrived) = refs[:6], refs[6:12], refs[12:]
    gain, x_all, weight_in, weight_out, scales, _ = near

    @pl.when(lax.axis_index("section") == 0)
    def _():
        copies = arrivals(far, near, arrived)
        for copy in copies:
            copy.start()
        copies[0].wait()
        copies[1].wait()
        x = x_all[0].astype(F32)
        normed_bf, _, _ = normalize(x, gain[...])
        in_tiles = tiles(weight_in.shape[1])
        for copy, cols in zip(copies[2:], in_tiles):
            copy.wait()
            acted[:, cols] = gelu(dot(normed_bf, weight_in[:, cols])).astype(BF16)
        for copy in copies[2 + len(in_tiles) :]:
            copy.wait()
        for cols in tiles(x.shape[1]):
            branch = dot(acted[...], weight_out[:, cols])
            out[:, cols] = (x[:, cols] + scales[:, cols] * branch).astype(BF16)


def load_kernel(*refs):
    far, near, arrived = refs[:6], refs[12:18], refs[18]

    @pl.when(lax.axis_index("section") != 0)
    def _():
        copies = arrivals(far, near, arrived)
        for copy in copies:
            copy.start()
        for copy in copies:
            copy.wait()


def turn_kernel(last, owner_table, weight_in, weight_out, scales, asked, turned_in, turned_out, owned, *ahead):
    device = lax.axis_index("dp")
    owned[0] = owner_table[device]
    owned[1] = owner_table[lax.min(device + 1 - 2 * lax.rem(device, 2), owner_table.shape[0] - 1)]
    for ref, turned in ((weight_in, turned_in), (weight_out, turned_out)):
        for rows in tiles(ref.shape[0]):
            for cols in tiles(ref.shape[1]):
                turned[cols, rows] = ref[rows, cols].T

    @pl.when(lax.axis_index("section") == last)
    def _():
        for batch, grad_act in enumerate(ahead):
            scaled = (asked[batch].astype(F32) * scales[...]).astype(BF16)
            for cols in tiles(turned_out.shape[1]):
                grad_act[:, cols] = dot(scaled, turned_out[:, cols])


def forward_kernel(step, batch, x_ref, gain, weight_in, weight_out, scales, out, acted):
    @pl.when(lax.axis_index("section") == step)
    def _():
        x = (x_ref[...] if batch is None else x_ref[batch]).astype(F32)
        normed_bf, _, _ = normalize(x, gain[...])
        for cols in tiles(weight_in.shape[1]):
            acted[:, cols] = gelu(dot(normed_bf, weight_in[:, cols])).astype(BF16)
        for cols in tiles(x.shape[1]):
            branch = dot(acted[...], weight_out[:, cols])
            out[:, cols] = (x[:, cols] + scales[:, cols] * branch).astype(BF16)


def choose(whole, batch, place, later, chosen):
    section = lax.axis_index("section")

    @pl.when(section == place)
    def _():
        chosen[...] = whole[batch]

    for index, ref in later:
        @pl.when(section == index)
        def _():
            chosen[...] = ref[...]


def save_kernel(batch, sections, *refs):
    whole, later, refs = refs[0], refs[1:sections], refs[sections:]
    gain, weight_in, normed_bf, normed, inv_std, slope, chosen = refs
    choose(whole, batch, 0, list(enumerate(later, 1)), chosen)
    normed_bf[...], normed[...], inv_std[...] = normalize(chosen[...].astype(F32), gain[...])
    for cols in tiles(weight_in.shape[1]):
        slope[:, cols] = gelu_slope(dot(normed_bf[...], weight_in[:, cols]))


def backward_kernel(
    step, batch, gy_ref, gain, turned_in, turned_out, scales, normed_ref, inv_std, slope, *refs
):
    *ahead, out, grad_hidden = refs

    @pl.when(lax.axis_index("section") == step)
    def _():
        cotangent = (gy_ref[...] if batch is None else gy_ref[batch]).astype(F32)
        scaled = (cotangent * scales[...]).astype(BF16)
        for cols in tiles(turned_out.shape[1]):
            grad_act = ahead[0][:, cols] if ahead else dot(scaled, turned_out[:, cols])
            grad_hidden[:, cols] = (grad_act * slope[:, cols]).astype(BF16)
        grad_normed = dot(grad_hidden[...], turned_in[...]) * gain[...]
        normed = normed_ref[...]
        mean_one = jnp.mean(grad_normed, axis=-1, keepdims=True)
        mean_two = jnp.mean(grad_normed * normed, axis=-1, keepdims=True)
        out[...] = (
            cotangent + inv_std[...] * (grad_normed - mean_one - normed * mean_two)
        ).astype(BF16)


def pick_kernel(batch, sections, *refs):
    whole, later, chosen = refs[0], refs[1:sections], refs[-1]
    choose(whole, batch, sections - 1, list(enumerate(later)), chosen)


def slopes_kernel(count, batches, owned, *refs):
    blocks, weight_in, known, refs = refs[:count], refs[count], refs[count + 1 :][:batches], refs[count + 1 + batches :]
    sums, slopes, rows = refs[:2], refs[2:-1], refs[-1]
    part = known[0].shape[0]
    for batch, slope in enumerate(slopes):
        slope[:part, :] = known[batch][...]
        others = jnp.concatenate([block[batch * part : (batch + 1) * part, :] for block in blocks[1:]], axis=0)
        for cols in tiles(weight_in.shape[1], 256):
            slope[part:, cols] = gelu_slope(dot(others, weight_in[:, cols]))
    height = blocks[0].shape[0]
    for index, block in enumerate(blocks):
        rows[index * height : (index + 1) * height, :] = block[...]
    for which, total in enumerate(sums):
        for cols, value in products([[rows]], owned[which], total.shape[0], tiles(total.shape[1])):
            total[:, cols] = value


def arrived_kernel(*refs):
    pass


def stack_kernel(*refs):
    *blocks, whole = refs
    height = blocks[0].shape[0]
    for index, block in enumerate(blocks):
        whole[index * height : (index + 1) * height, :] = block[...]


def hidden_kernel(count, columns, *refs):
    blocks, (scales, turned_out, slope, grad_hidden, scaled) = refs[:count], refs[count:]
    first = columns.start
    part = blocks[0].shape[0]
    for index, block in enumerate(blocks):
        scaled[index * part : (index + 1) * part, :] = (
            block[...].astype(F32) * scales[...]
        ).astype(BF16)
    for cols in tiles(columns.stop - first, 256):
        there = slice(first + cols.start, first + cols.stop)
        grad_act = dot(scaled[...], turned_out[:, there])
        grad_hidden[:, cols] = (grad_act * slope[:, there]).astype(BF16)


def products(blocks, owner, tall, pieces, earlier=None):
    own = []
    for parts in blocks:
        each = parts[0].shape[1] // tall
        mine = pl.ds(pl.multiple_of(lax.rem(owner, each) * tall, tall), tall)
        value = parts[0][:, mine].T
        for index, part in enumerate(parts[1:], 1):
            value = jnp.where(lax.div(owner, each) == index, part[:, mine].T, value)
        own.append(value)
    for cols in pieces:
        value = None if earlier is None else earlier[:, cols]
        for mine_turned, parts in zip(own, blocks):
            width = parts[0].shape[1]
            first = cols.start // width
            there = slice(cols.start - first * width, cols.stop - first * width)
            term = dot(mine_turned, parts[first][:, there])
            value = term if value is None else value + term
        yield cols, value


def grouped(counts, refs):
    blocks = []
    for count in counts:
        blocks.append(refs[:count])
        refs = refs[count:]
    return blocks, refs


def square_kernel(counts, factor, owned, *refs):
    blocks, (earlier, total, stage, left) = grouped(counts, refs)
    tall, width = stage.shape
    copies = []
    for cols, value in products(blocks, owned[0], tall, tiles(width, 256), earlier):
        stage[:, cols] = value * factor
        copies.append(pltpu.make_async_copy(stage.at[:, cols], total.at[:, cols], left.at[len(copies)]))
        copies[-1].start()
    for copy in copies:
        copy.wait()


def partial_kernel(counts, factor, owned, *refs):
    blocks, (mine, other, total, act_share, stage, left) = grouped(counts, refs)
    stage[...] = (mine[...] + other[...]) * factor
    copy = pltpu.make_async_copy(stage, act_share, left.at[0])
    copy.start()
    for cols, value in products(blocks, owned[0], total.shape[0], tiles(total.shape[1], 256)):
        total[:, cols] = value
    copy.wait()


def pinned(value):
    return pltpu.with_memory_space_constraint(value, pltpu.VMEM)


def shape(dims, dtype=BF16):
    return jax.ShapeDtypeStruct(dims, dtype)


class Order:
    def __init__(self):
        self.token = []

    def __call__(
        self, kernel, arrays, outs, scratch=(), flops=0, specs=None, name=None, aliases=None, out_specs=None, ordered=True, free=False
    ):
        count, before = len(arrays), [] if free else self.token

        def body(*refs):
            given, rest = refs[:count], refs[count + len(before) :]
            kernel(*given, *rest[: len(outs)], *rest[len(outs) + ordered :])

        results = pl.pallas_call(
            body,
            in_specs=(specs or [IN_VMEM] * count) + [IN_VMEM] * len(before),
            out_specs=(out_specs or [IN_VMEM] * len(outs)) + [IN_VMEM] * ordered,
            out_shape=[*outs] + [pltpu.VMEM((8, 128), F32)] * ordered,
            scratch_shapes=list(scratch),
            input_output_aliases=aliases or {},
            compiler_params=pltpu.CompilerParams(vmem_limit_bytes=ROOM),
            cost_estimate=pl.CostEstimate(flops=flops, bytes_accessed=8 * MIB, transcendentals=0),
            name=name,
        )(*arrays, *before)
        if ordered:
            self.token = [pinned(results[-1])]
            return results[:-1]
        return results


def stack(call, blocks):
    height, width = blocks[0].shape
    outs = [shape((height * len(blocks), width), blocks[0].dtype)]
    return call(stack_kernel, [pinned(block) for block in blocks], outs, name="stack", ordered=False, free=True)[0]


def owned_partial(call, blocks, owned, owners, factor, act_parts):
    width = sum(part.shape[1] for part in blocks[0])
    parts = [pinned(part) for block in blocks for part in block]
    act = shape(act_parts[0].shape, F32)
    return call(
        functools.partial(partial_kernel, [len(block) for block in blocks], factor),
        [owned, *parts, *[pinned(value) for value in act_parts]],
        [shape((width // owners, width), F32), act],
        [pltpu.VMEM(act.shape, F32), pltpu.SemaphoreType.DMA((1,))],
        specs=[IN_SMEM] + [IN_VMEM] * (len(parts) + 2),
        name="partial",
        out_specs=[IN_VMEM, pl.BlockSpec(memory_space=pltpu.HBM)],
        ordered=False,
    )


def owned_square(call, blocks, owned, owners, factor, earlier):
    width = sum(part.shape[1] for part in blocks[0])
    tall = width // owners
    parts = [pinned(part) for block in blocks for part in block]
    return call(
        functools.partial(square_kernel, [len(block) for block in blocks], factor),
        [owned, *parts, pinned(earlier)],
        [shape((tall, width), F32)],
        [pltpu.VMEM((tall, width), F32), pltpu.SemaphoreType.DMA((len(tiles(width, 256)),))],
        specs=[IN_SMEM] + [IN_VMEM] * (len(parts) + 1),
        name="square",
        out_specs=[pl.BlockSpec(memory_space=pltpu.HBM)],
        ordered=False,
    )[0]


def plain_square(rows, owner_table, owners, total_rows):
    everything = lax.all_gather(rows, "dp", axis=0, tiled=True)
    tall = rows.shape[1] // owners
    start = owner_table[lax.axis_index("dp")] * tall
    own = lax.dynamic_slice_in_dim(everything, start, tall, axis=1)
    return dot_tn(own, everything) / total_rows


def body(inputs, ln_gain, w_in, w_out, layer_scale, out_grad, owner_table):
    sections = lax.axis_size("section")
    owners = lax.axis_size("dp")
    batch_count, row_count, width = inputs.shape
    width_hidden = w_in.shape[2]
    total_rows = batch_count * row_count * owners
    batches = range(batch_count)
    product = 2 * row_count * width * width_hidden
    block = shape((row_count, width))
    wide = pltpu.VMEM((row_count, width_hidden), BF16)
    flat = pltpu.VMEM((row_count, width), BF16)
    far = [ln_gain, inputs, w_in, w_out, layer_scale, out_grad]
    sizes = [ln_gain.shape, inputs.shape, w_in.shape[1:], w_out.shape[1:], ln_gain.shape, inputs.shape]
    homes = [pltpu.VMEM(size, value.dtype) for size, value in zip(sizes, far)]
    far = [pltpu.with_memory_space_constraint(value, pltpu.HBM) for value in far]
    far_specs = [pl.BlockSpec(memory_space=pltpu.HBM)] * len(far)
    flags = pltpu.SemaphoreType.DMA((4 + 2 * len(tiles(width_hidden)),))
    call = Order()
    *near, output = call(
        first_kernel, far, homes + [block], [wide, flags], 2 * product, far_specs, "first"
    )
    arrived = [[pinned(hop(output, 0, 1))]] + [[] for m in batches[1:]]
    near = call(
        load_kernel,
        far + [pinned(value) for value in near],
        homes,
        [flags],
        specs=far_specs + [IN_VMEM] * len(near),
        name="load",
        aliases={len(far) + index: index for index in range(len(far))},
    )
    paired = owners in (2, 4, 8) and not (width // owners % 128 or width_hidden // owners % 128)
    masks = range(2, owners, 2)
    gain, given, weight_in, weight_out, scales, asked = [pinned(value) for value in near]
    for step in range(sections - 1):
        for m in batches:
            if not (step or m):
                continue
            (output,) = call(
                functools.partial(forward_kernel, step, None if step else m),
                [arrived[m][-1] if step else given, gain, weight_in, weight_out, scales],
                [block],
                [wide],
                2 * product,
                name="forward",
            )
            arrived[m].append(pinned(hop(output, step, 1)))
        if step == 0:
            turned_in, turned_out, owned, *ahead = call(
                functools.partial(turn_kernel, sections - 1),
                [owner_table, weight_in, weight_out, scales, asked],
                [
                    pltpu.VMEM((width_hidden, width), BF16),
                    pltpu.VMEM((width, width_hidden), BF16),
                    pltpu.SMEM((2,), jnp.int32),
                ]
                + [shape((row_count, width_hidden), F32)] * batch_count,
                name="turn",
                specs=[IN_SMEM] + [IN_VMEM] * 4,
                out_specs=[IN_VMEM, IN_VMEM, IN_SMEM] + [IN_VMEM] * batch_count,
            )
            owned = pltpu.with_memory_space_constraint(owned, pltpu.SMEM)
            turned_in, turned_out = pinned(turned_in), pinned(turned_out)

    saved, returned = [], [[] for m in batches]
    for step in range(sections - 1, 0, -1):
        for m in batches:
            if paired and step == 1 and m == batches[-1]:
                call(arrived_kernel, [pinned(x) for x in gathered], [], name="arrived")
            if len(saved) <= m:
                values = call(
                    functools.partial(save_kernel, m, sections),
                    [given, *arrived[m], gain, weight_in],
                    [
                        block,
                        shape((row_count, width), F32),
                        shape((row_count, 1), F32),
                        shape((row_count, width_hidden), F32),
                    ],
                    [flat],
                    product,
                    name="save",
                )
                saved.append([pinned(value) for value in values])
            (grad_input,) = call(
                functools.partial(backward_kernel, step, m if step == sections - 1 else None),
                [
                    asked if step == sections - 1 else returned[m][0],
                    gain, turned_in, turned_out, scales, *saved[m][1:],
                    *([pinned(ahead[m])] if step == sections - 1 else []),
                ],
                [block],
                [wide],
                2 * product,
                name="backward",
            )
            returned[m].insert(0, pinned(hop(grad_input, step, -1)))
        if step == sections - 1:
            merged = stack(call, [saved[m][0] for m in batches])
            if paired:
                gathered = [merged] + [swapped(merged, "dp", mask) for mask in masks]
                count = len(gathered)
    factor = 1.0 / total_rows
    if paired:
        tall = width // owners
        sums = [shape((tall, width), F32)] * 2
        own, other, *slopes = call(
            functools.partial(slopes_kernel, count, batch_count),
            [owned, *[pinned(x) for x in gathered], weight_in, *[saved[m][3] for m in batches]],
            [*sums, *[shape((count * row_count, width_hidden), F32)] * batch_count],
            [pltpu.VMEM((count * batch_count * row_count, width), BF16)],
            specs=[IN_SMEM] + [IN_VMEM] * (count + 1 + batch_count),
            name="slopes",
        )
        other = swapped(other, "dp", 1)
    hidden_blocks, cotangents = [], []
    for m in batches:
        (cotangent,) = call(
            functools.partial(pick_kernel, m, sections),
            [asked, *returned[m]],
            [block],
            name="pick",
            ordered=False,
        )
        cotangents.append(cotangent)
    for m in batches:
        cotangent = cotangents[m]
        near = [cotangent] + [swapped(cotangent, "dp", mask) for mask in masks if paired]
        count = len(near)
        parts = tiles(width_hidden, width_hidden // 2 if paired else width_hidden)
        made = [
            call(
                functools.partial(hidden_kernel, count, columns),
                [*[pinned(x) for x in near], scales, turned_out, pinned(slopes[m]) if paired else saved[m][3]],
                [shape((count * row_count, columns.stop - columns.start))],
                [pltpu.VMEM((count * row_count, width), BF16)],
                product * count // len(parts),
                name="hidden",
                ordered=False,
            )[0]
            for columns in parts
        ]
        hidden_blocks.append(made)
        if paired:
            hidden_blocks.append([swapped(part, "dp", 1) for part in made])
    if not paired:
        grad_rows = jnp.concatenate([made[0] for made in hidden_blocks], axis=0)
        return (
            plain_square(merged, owner_table, owners, total_rows)[None],
            plain_square(grad_rows, owner_table, owners, total_rows)[None],
        )
    earlier, act_share = owned_partial(call, hidden_blocks[:-1], owned, owners, factor, [own, other])
    grad_share = owned_square(call, hidden_blocks[-1:], owned, owners, factor, earlier)
    return (act_share[None], grad_share[None])


def solution(mesh):
    placed = (
        P(None, "dp", None),
        P("section", None),
        P("section", None, None),
        P("section", None, None),
        P("section", None),
        P(None, "dp", None),
        P(),
    )
    return jax.shard_map(
        body,
        mesh=mesh,
        in_specs=placed,
        out_specs=(P("section", "dp", None), P("section", "dp", None)),
        check_vma=False,
    )
```

```python
import functools

import jax
import jax.numpy as jnp
from jax import lax
from jax.experimental import pallas as pl
from jax.experimental.pallas import tpu as pltpu
from jax.sharding import PartitionSpec as P

SQRT_HALF = 0.7071067811865476
INV_ROOT_TAU = 0.3989422804014327
F32 = jnp.float32
BF16 = jnp.bfloat16
IN_VMEM = pl.BlockSpec(memory_space=pltpu.VMEM)
IN_SMEM = pl.BlockSpec(memory_space=pltpu.SMEM)
TILE = 512
MIB = 2**20
ROOM = 24 * MIB


def hop(value, source, steps):
    return lax.ppermute(value, "section", [(source, source + steps)])


def swapped(value, axis, mask):
    count = lax.axis_size(axis)
    return lax.ppermute(value, axis, [(source, source ^ mask) for source in range(count)])


def tiles(width, most=TILE):
    size = min(most, width)
    return [slice(start, min(start + size, width)) for start in range(0, width, size)]


def dot(left, right):
    return jnp.dot(left, right, preferred_element_type=F32)


def dot_tn(left, right):
    return lax.dot_general(left, right, (((0,), (0,)), ((), ())), preferred_element_type=F32)


def normalize(floats, gain_row):
    center = floats - jnp.mean(floats, axis=-1, keepdims=True)
    inv_std = lax.rsqrt(jnp.mean(center * center, axis=-1, keepdims=True) + 1e-06)
    normed = center * inv_std
    return ((normed * gain_row).astype(BF16), normed, inv_std)


def gelu(v):
    return 0.5 * v * (1.0 + lax.erf(v * SQRT_HALF))


def gelu_slope(v):
    return 0.5 * (1.0 + lax.erf(v * SQRT_HALF)) + v * INV_ROOT_TAU * jnp.exp(-0.5 * v * v)


def arrivals(far, near, arrived):
    gain, x_all, weight_in, weight_out, scales, asked = near
    pairs = [(far[0], gain), (far[1], x_all)]
    pairs += [(far[2].at[0, :, cols], weight_in.at[:, cols]) for cols in tiles(weight_in.shape[1])]
    pairs += [(far[3].at[0, rows, :], weight_out.at[rows, :]) for rows in tiles(weight_out.shape[0])]
    pairs += [(far[4], scales), (far[5], asked)]
    return [
        pltpu.make_async_copy(source, target, arrived.at[index])
        for index, (source, target) in enumerate(pairs)
    ]


def first_kernel(*refs):
    far, near, (out, acted, arrived) = refs[:6], refs[6:12], refs[12:]
    gain, x_all, weight_in, weight_out, scales, _ = near

    @pl.when(lax.axis_index("section") == 0)
    def _():
        copies = arrivals(far, near, arrived)
        for copy in copies:
            copy.start()
        copies[0].wait()
        copies[1].wait()
        x = x_all[0].astype(F32)
        normed_bf, _, _ = normalize(x, gain[...])
        in_tiles = tiles(weight_in.shape[1])
        for copy, cols in zip(copies[2:], in_tiles):
            copy.wait()
            acted[:, cols] = gelu(dot(normed_bf, weight_in[:, cols])).astype(BF16)
        branch = None
        for copy, rows in zip(copies[2 + len(in_tiles) :], tiles(weight_out.shape[0])):
            copy.wait()
            term = dot(acted[:, rows], weight_out[rows, :])
            branch = term if branch is None else branch + term
        for copy in copies[-2:]:
            copy.wait()
        out[...] = (x + scales[...] * branch).astype(BF16)


def load_kernel(*refs):
    far, near, arrived = refs[:6], refs[12:18], refs[18]

    @pl.when(lax.axis_index("section") != 0)
    def _():
        copies = arrivals(far, near, arrived)
        for copy in copies:
            copy.start()
        for copy in copies:
            copy.wait()


def turn_kernel(last, owner_table, weight_in, weight_out, scales, asked, turned_in, turned_out, owned, *ahead):
    device = lax.axis_index("dp")
    owned[0] = owner_table[device]
    owned[1] = owner_table[lax.min(device + 1 - 2 * lax.rem(device, 2), owner_table.shape[0] - 1)]
    for ref, turned in ((weight_in, turned_in), (weight_out, turned_out)):
        for rows in tiles(ref.shape[0]):
            for cols in tiles(ref.shape[1]):
                turned[cols, rows] = ref[rows, cols].T

    @pl.when(lax.axis_index("section") == last)
    def _():
        for batch, grad_act in enumerate(ahead):
            scaled = (asked[batch].astype(F32) * scales[...]).astype(BF16)
            for cols in tiles(turned_out.shape[1]):
                grad_act[:, cols] = dot(scaled, turned_out[:, cols])


def forward_kernel(step, batch, x_ref, gain, weight_in, weight_out, scales, out, acted):
    @pl.when(lax.axis_index("section") == step)
    def _():
        x = (x_ref[...] if batch is None else x_ref[batch]).astype(F32)
        normed_bf, _, _ = normalize(x, gain[...])
        for cols in tiles(weight_in.shape[1]):
            acted[:, cols] = gelu(dot(normed_bf, weight_in[:, cols])).astype(BF16)
        for cols in tiles(x.shape[1]):
            branch = dot(acted[...], weight_out[:, cols])
            out[:, cols] = (x[:, cols] + scales[:, cols] * branch).astype(BF16)


def choose(whole, batch, place, later, chosen):
    section = lax.axis_index("section")

    @pl.when(section == place)
    def _():
        chosen[...] = whole[batch]

    for index, ref in later:
        @pl.when(section == index)
        def _():
            chosen[...] = ref[...]


def save_kernel(batch, sections, *refs):
    whole, later, refs = refs[0], refs[1:sections], refs[sections:]
    gain, weight_in, normed_bf, normed, inv_std, slope, chosen = refs
    choose(whole, batch, 0, list(enumerate(later, 1)), chosen)
    normed_bf[...], normed[...], inv_std[...] = normalize(chosen[...].astype(F32), gain[...])
    for cols in tiles(weight_in.shape[1]):
        slope[:, cols] = gelu_slope(dot(normed_bf[...], weight_in[:, cols]))


def backward_kernel(
    step, batch, gy_ref, gain, turned_in, turned_out, scales, normed_ref, inv_std, slope, *refs
):
    *ahead, out, grad_hidden = refs

    @pl.when(lax.axis_index("section") == step)
    def _():
        cotangent = (gy_ref[...] if batch is None else gy_ref[batch]).astype(F32)
        scaled = (cotangent * scales[...]).astype(BF16)
        for cols in tiles(turned_out.shape[1]):
            grad_act = ahead[0][:, cols] if ahead else dot(scaled, turned_out[:, cols])
            grad_hidden[:, cols] = (grad_act * slope[:, cols]).astype(BF16)
        grad_normed = dot(grad_hidden[...], turned_in[...]) * gain[...]
        normed = normed_ref[...]
        mean_one = jnp.mean(grad_normed, axis=-1, keepdims=True)
        mean_two = jnp.mean(grad_normed * normed, axis=-1, keepdims=True)
        out[...] = (
            cotangent + inv_std[...] * (grad_normed - mean_one - normed * mean_two)
        ).astype(BF16)


def pick_kernel(batch, sections, *refs):
    whole, later, chosen = refs[0], refs[1:sections], refs[-1]
    choose(whole, batch, sections - 1, list(enumerate(later)), chosen)


def take_slopes(section, count, *refs):
    batches = (len(refs) - count - 1) // 2
    blocks, weight_in, known, slopes = refs[:count], refs[count], refs[count + 1 : -batches], refs[-batches:]
    part = known[0].shape[0]

    @pl.when(section(lax.axis_index("section")))
    def _():
        size = (count - 1) * part
        others = [block[batch * part : (batch + 1) * part, :] for batch in range(batches) for block in blocks[1:]]
        others = jnp.concatenate(others, axis=0)
        for cols in tiles(weight_in.shape[1], 256):
            values = gelu_slope(dot(others, weight_in[:, cols]))
            for batch, slope in enumerate(slopes):
                slope[part:, cols] = values[batch * size : (batch + 1) * size, :]
        for batch, slope in enumerate(slopes):
            slope[:part, :] = known[batch][...]


def slopes_kernel(count, batches, late, owned, *refs):
    sums, slopes, rows = refs[count + 1 + batches :][:2], refs[-1 - batches : -1], refs[-1]
    take_slopes(lambda section: section != late, count, *refs[: count + 1 + batches], *slopes)
    blocks = refs[:count]
    height = blocks[0].shape[0]
    for index, block in enumerate(blocks):
        rows[index * height : (index + 1) * height, :] = block[...]
    for which, total in enumerate(sums):
        for cols, value in products([rows], owned[which], total.shape[0], tiles(total.shape[1])):
            total[:, cols] = value


def late_kernel(count, batches, late, *refs):
    take_slopes(lambda section: section == late, count, *refs[: count + 1 + batches], *refs[-batches:])


def arrived_kernel(*refs):
    pass


def stack_kernel(*refs):
    *blocks, whole = refs
    height = blocks[0].shape[0]
    for index, block in enumerate(blocks):
        whole[index * height : (index + 1) * height, :] = block[...]


def hidden_kernel(places, *refs):
    count = len(places)
    blocks, (scales, turned_out, slope, grad_hidden, scaled) = refs[:count], refs[count:]
    part = blocks[0].shape[0]
    for index, block in enumerate(blocks):
        scaled[index * part : (index + 1) * part, :] = (
            block[...].astype(F32) * scales[...]
        ).astype(BF16)
    for cols in tiles(turned_out.shape[1], 256):
        grad_act = dot(scaled[...], turned_out[:, cols])
        for index, place in enumerate(places):
            rows = slice(index * part, (index + 1) * part)
            there = slope[place * part : (place + 1) * part, cols]
            grad_hidden[rows, cols] = (grad_act[rows, :] * there).astype(BF16)


def products(blocks, owner, tall, pieces, earlier=None):
    mine = pl.ds(pl.multiple_of(owner * tall, tall), tall)
    for cols in pieces:
        own = jnp.concatenate([block[:, mine] for block in blocks], axis=0)
        value = dot_tn(own, jnp.concatenate([block[:, cols] for block in blocks], axis=0))
        yield cols, value if earlier is None else earlier[:, cols] + value


def square_kernel(count, factor, owned, *refs):
    blocks, (earlier, total, stage, left) = refs[:count], refs[count:]
    tall, width = stage.shape
    copies = []
    for cols, value in products(blocks, owned[0], tall, tiles(width), earlier):
        stage[:, cols] = value * factor
        copies.append(pltpu.make_async_copy(stage.at[:, cols], total.at[:, cols], left.at[len(copies)]))
        copies[-1].start()
    for copy in copies:
        copy.wait()


def partial_kernel(count, factor, owned, *refs):
    blocks, (mine, other, total, act_share, stage, left) = refs[:count], refs[count:]
    stage[...] = (mine[...] + other[...]) * factor
    copy = pltpu.make_async_copy(stage, act_share, left.at[0])
    copy.start()
    for cols, value in products(blocks, owned[0], total.shape[0], tiles(total.shape[1])):
        total[:, cols] = value
    copy.wait()


def pinned(value):
    return pltpu.with_memory_space_constraint(value, pltpu.VMEM)


def shape(dims, dtype=BF16):
    return jax.ShapeDtypeStruct(dims, dtype)


class Order:
    def __init__(self):
        self.token = []

    def __call__(
        self, kernel, arrays, outs, scratch=(), flops=0, specs=None, name=None, aliases=None, out_specs=None, ordered=True, free=False
    ):
        count, before = len(arrays), [] if free else self.token

        def body(*refs):
            given, rest = refs[:count], refs[count + len(before) :]
            kernel(*given, *rest[: len(outs)], *rest[len(outs) + ordered :])

        results = pl.pallas_call(
            body,
            in_specs=(specs or [IN_VMEM] * count) + [IN_VMEM] * len(before),
            out_specs=(out_specs or [IN_VMEM] * len(outs)) + [IN_VMEM] * ordered,
            out_shape=[*outs] + [pltpu.VMEM((8, 128), F32)] * ordered,
            scratch_shapes=list(scratch),
            input_output_aliases=aliases or {},
            compiler_params=pltpu.CompilerParams(vmem_limit_bytes=ROOM),
            cost_estimate=pl.CostEstimate(flops=flops, bytes_accessed=8 * MIB, transcendentals=0),
            name=name,
        )(*arrays, *before)
        if ordered:
            self.token = [pinned(results[-1])]
            return results[:-1]
        return results


def stack(call, blocks):
    height, width = blocks[0].shape
    outs = [shape((height * len(blocks), width), blocks[0].dtype)]
    return call(stack_kernel, [pinned(block) for block in blocks], outs, name="stack", ordered=False, free=True)[0]


def owned_partial(call, blocks, owned, owners, factor, act_parts):
    width = blocks[0].shape[1]
    act = shape(act_parts[0].shape, F32)
    return call(
        functools.partial(partial_kernel, len(blocks), factor),
        [owned, *[pinned(value) for value in [*blocks, *act_parts]]],
        [shape((width // owners, width), F32), act],
        [pltpu.VMEM(act.shape, F32), pltpu.SemaphoreType.DMA((1,))],
        specs=[IN_SMEM] + [IN_VMEM] * (len(blocks) + 2),
        name="partial",
        out_specs=[IN_VMEM, pl.BlockSpec(memory_space=pltpu.HBM)],
        ordered=False,
    )


def owned_square(call, blocks, owned, owners, factor, earlier):
    width = blocks[0].shape[1]
    tall = width // owners
    return call(
        functools.partial(square_kernel, len(blocks), factor),
        [owned, *[pinned(value) for value in [*blocks, earlier]]],
        [shape((tall, width), F32)],
        [pltpu.VMEM((tall, width), F32), pltpu.SemaphoreType.DMA((len(tiles(width, 256)),))],
        specs=[IN_SMEM] + [IN_VMEM] * (len(blocks) + 1),
        name="square",
        out_specs=[pl.BlockSpec(memory_space=pltpu.HBM)],
        ordered=False,
    )[0]


def plain_square(rows, owner_table, owners, total_rows):
    everything = lax.all_gather(rows, "dp", axis=0, tiled=True)
    tall = rows.shape[1] // owners
    start = owner_table[lax.axis_index("dp")] * tall
    own = lax.dynamic_slice_in_dim(everything, start, tall, axis=1)
    return dot_tn(own, everything) / total_rows


def body(inputs, ln_gain, w_in, w_out, layer_scale, out_grad, owner_table):
    sections = lax.axis_size("section")
    owners = lax.axis_size("dp")
    batch_count, row_count, width = inputs.shape
    width_hidden = w_in.shape[2]
    total_rows = batch_count * row_count * owners
    batches = range(batch_count)
    product = 2 * row_count * width * width_hidden
    block = shape((row_count, width))
    wide = pltpu.VMEM((row_count, width_hidden), BF16)
    flat = pltpu.VMEM((row_count, width), BF16)
    far = [ln_gain, inputs, w_in, w_out, layer_scale, out_grad]
    sizes = [ln_gain.shape, inputs.shape, w_in.shape[1:], w_out.shape[1:], ln_gain.shape, inputs.shape]
    homes = [pltpu.VMEM(size, value.dtype) for size, value in zip(sizes, far)]
    far = [pltpu.with_memory_space_constraint(value, pltpu.HBM) for value in far]
    far_specs = [pl.BlockSpec(memory_space=pltpu.HBM)] * len(far)
    flags = pltpu.SemaphoreType.DMA((4 + 2 * len(tiles(width_hidden)),))
    call = Order()
    *near, output = call(
        first_kernel, far, homes + [block], [wide, flags], 2 * product, far_specs, "first"
    )
    arrived = [[pinned(hop(output, 0, 1))]] + [[] for m in batches[1:]]
    near = call(
        load_kernel,
        far + [pinned(value) for value in near],
        homes,
        [flags],
        specs=far_specs + [IN_VMEM] * len(near),
        name="load",
        aliases={len(far) + index: index for index in range(len(far))},
    )
    paired = owners in (2, 4, 8) and not (width // owners % 128 or width_hidden // owners % 128)
    masks = range(2, owners, 2)
    gain, given, weight_in, weight_out, scales, asked = [pinned(value) for value in near]
    for step in range(sections - 1):
        for m in batches:
            if not (step or m):
                continue
            (output,) = call(
                functools.partial(forward_kernel, step, None if step else m),
                [arrived[m][-1] if step else given, gain, weight_in, weight_out, scales],
                [block],
                [wide],
                2 * product,
                name="forward",
            )
            arrived[m].append(pinned(hop(output, step, 1)))
        if step == min(1, sections - 2):
            turned_in, turned_out, owned, *ahead = call(
                functools.partial(turn_kernel, sections - 1),
                [owner_table, weight_in, weight_out, scales, asked],
                [
                    pltpu.VMEM((width_hidden, width), BF16),
                    pltpu.VMEM((width, width_hidden), BF16),
                    pltpu.SMEM((2,), jnp.int32),
                ]
                + [shape((row_count, width_hidden), F32)] * batch_count,
                name="turn",
                specs=[IN_SMEM] + [IN_VMEM] * 4,
                out_specs=[IN_VMEM, IN_VMEM, IN_SMEM] + [IN_VMEM] * batch_count,
            )
            owned = pltpu.with_memory_space_constraint(owned, pltpu.SMEM)
            turned_in, turned_out = pinned(turned_in), pinned(turned_out)

    saved, returned = [], [[] for m in batches]
    for step in range(sections - 1, 0, -1):
        for m in batches:
            if paired and step == 1 and m == batches[-1]:
                call(arrived_kernel, [pinned(x) for x in gathered], [], name="arrived")
            if len(saved) <= m:
                values = call(
                    functools.partial(save_kernel, m, sections),
                    [given, *arrived[m], gain, weight_in],
                    [
                        block,
                        shape((row_count, width), F32),
                        shape((row_count, 1), F32),
                        shape((row_count, width_hidden), F32),
                    ],
                    [flat],
                    product,
                    name="save",
                )
                saved.append([pinned(value) for value in values])
            (grad_input,) = call(
                functools.partial(backward_kernel, step, m if step == sections - 1 else None),
                [
                    asked if step == sections - 1 else returned[m][0],
                    gain, turned_in, turned_out, scales, *saved[m][1:],
                    *([pinned(ahead[m])] if step == sections - 1 else []),
                ],
                [block],
                [wide],
                2 * product,
                name="backward",
            )
            returned[m].insert(0, pinned(hop(grad_input, step, -1)))
        if step == sections - 1:
            merged = stack(call, [saved[m][0] for m in batches])
            if paired:
                gathered = [merged] + [swapped(merged, "dp", mask) for mask in masks]
                count = len(gathered)
    factor = 1.0 / total_rows
    if paired:
        tall = width // owners
        sums = [shape((tall, width), F32)] * 2
        to_slopes = [*[pinned(x) for x in gathered], weight_in, *[saved[m][3] for m in batches]]
        own, other, *slopes = call(
            functools.partial(slopes_kernel, count, batch_count, 1),
            [owned, *to_slopes],
            [*sums, *[shape((count * row_count, width_hidden), F32)] * batch_count],
            [pltpu.VMEM((count * batch_count * row_count, width), BF16)],
            specs=[IN_SMEM] + [IN_VMEM] * (count + 1 + batch_count),
            name="slopes",
        )
        other = swapped(other, "dp", 1)
    hidden_blocks, cotangents = [], []
    for m in batches:
        (cotangent,) = call(
            functools.partial(pick_kernel, m, sections),
            [asked, *returned[m]],
            [block],
            name="pick",
            ordered=m == 0,
        )
        cotangents.append(cotangent)
        if paired and m == 0:
            slopes = call(
                functools.partial(late_kernel, count, batch_count, 1),
                [*to_slopes, *[pinned(value) for value in slopes]],
                [shape((count * row_count, width_hidden), F32)] * batch_count,
                name="late",
                aliases={len(to_slopes) + n: n for n in batches},
                )
    for m in batches:
        cotangent = cotangents[m]
        order = [mask for mask in masks if paired]
        sent = {mask: swapped(cotangent, "dp", mask) for mask in (order if m else reversed(order))}
        near = [cotangent] + [sent[mask] for mask in order]
        count = len(near)
        places = [[0, *range(3, count)], list(range(1, min(count, 3)))] if count > 1 else [[0]]
        made = [
            call(
                functools.partial(hidden_kernel, part),
                [
                    *[pinned(near[place]) for place in part],
                    scales, turned_out, pinned(slopes[m]) if paired else saved[m][3],
                ],
                [shape((len(part) * row_count, width_hidden))],
                [pltpu.VMEM((len(part) * row_count, width), BF16)],
                name="hidden",
                ordered=False,
            )[0]
            for part in places
        ]
        hidden_blocks += made
        if paired:
            crossed = [swapped(part, "dp", 1) for part in made]
            hidden_blocks += crossed
    if not paired:
        grad_rows = jnp.concatenate(hidden_blocks, axis=0)
        return (
            plain_square(merged, owner_table, owners, total_rows)[None],
            plain_square(grad_rows, owner_table, owners, total_rows)[None],
        )
    late = len(crossed)
    earlier, act_share = owned_partial(call, hidden_blocks[:-late], owned, owners, factor, [own, other])
    grad_share = owned_square(call, hidden_blocks[-late:], owned, owners, factor, earlier)
    return (act_share[None], grad_share[None])


def solution(mesh):
    placed = (
        P(None, "dp", None),
        P("section", None),
        P("section", None, None),
        P("section", None, None),
        P("section", None),
        P(None, "dp", None),
        P(),
    )
    return jax.shard_map(
        body,
        mesh=mesh,
        in_specs=placed,
        out_specs=(P("section", "dp", None), P("section", "dp", None)),
        check_vma=False,
    )
```

```python
import functools

import jax
import jax.numpy as jnp
from jax import lax
from jax.experimental import pallas as pl
from jax.experimental.pallas import tpu as pltpu
from jax.sharding import PartitionSpec as P

SQRT_HALF = 0.7071067811865476
INV_ROOT_TAU = 0.3989422804014327
F32 = jnp.float32
BF16 = jnp.bfloat16
IN_VMEM = pl.BlockSpec(memory_space=pltpu.VMEM)
IN_SMEM = pl.BlockSpec(memory_space=pltpu.SMEM)
TILE = 512
MIB = 2**20
ROOM = 24 * MIB


def hop(value, source, steps):
    return lax.ppermute(value, "section", [(source, source + steps)])


def swapped(value, axis, mask):
    count = lax.axis_size(axis)
    return lax.ppermute(value, axis, [(source, source ^ mask) for source in range(count)])


def tiles(width, most=TILE):
    size = min(most, width)
    return [slice(start, min(start + size, width)) for start in range(0, width, size)]


def dot(left, right):
    return jnp.dot(left, right, preferred_element_type=F32)


def dot_tn(left, right):
    return lax.dot_general(left, right, (((0,), (0,)), ((), ())), preferred_element_type=F32)


def normalize(floats, gain_row):
    center = floats - jnp.mean(floats, axis=-1, keepdims=True)
    inv_std = lax.rsqrt(jnp.mean(center * center, axis=-1, keepdims=True) + 1e-06)
    normed = center * inv_std
    return ((normed * gain_row).astype(BF16), normed, inv_std)


def gelu(v):
    return 0.5 * v * (1.0 + lax.erf(v * SQRT_HALF))


def gelu_slope(v):
    return 0.5 * (1.0 + lax.erf(v * SQRT_HALF)) + v * INV_ROOT_TAU * jnp.exp(-0.5 * v * v)


def arrivals(far, near, arrived):
    gain, x_all, weight_in, weight_out, scales, asked = near
    pairs = [(far[0], gain), (far[1], x_all)]
    pairs += [(far[2].at[0, :, cols], weight_in.at[:, cols]) for cols in tiles(weight_in.shape[1])]
    pairs += [(far[3].at[0, rows, :], weight_out.at[rows, :]) for rows in tiles(weight_out.shape[0])]
    pairs += [(far[4], scales), (far[5], asked)]
    return [
        pltpu.make_async_copy(source, target, arrived.at[index])
        for index, (source, target) in enumerate(pairs)
    ]


def first_kernel(*refs):
    far, near, (out, acted, arrived) = refs[:6], refs[6:12], refs[12:]
    gain, x_all, weight_in, weight_out, scales, _ = near

    @pl.when(lax.axis_index("section") == 0)
    def _():
        copies = arrivals(far, near, arrived)
        for copy in copies:
            copy.start()
        copies[0].wait()
        copies[1].wait()
        x = x_all[0].astype(F32)
        normed_bf, _, _ = normalize(x, gain[...])
        in_tiles = tiles(weight_in.shape[1])
        for copy, cols in zip(copies[2:], in_tiles):
            copy.wait()
            acted[:, cols] = gelu(dot(normed_bf, weight_in[:, cols])).astype(BF16)
        branch = None
        for copy, rows in zip(copies[2 + len(in_tiles) :], tiles(weight_out.shape[0])):
            copy.wait()
            term = dot(acted[:, rows], weight_out[rows, :])
            branch = term if branch is None else branch + term
        for copy in copies[-2:]:
            copy.wait()
        out[...] = (x + scales[...] * branch).astype(BF16)


def load_kernel(*refs):
    far, near, arrived = refs[:6], refs[12:18], refs[18]

    @pl.when(lax.axis_index("section") != 0)
    def _():
        copies = arrivals(far, near, arrived)
        for copy in copies:
            copy.start()
        for copy in copies:
            copy.wait()


def turn_kernel(last, owner_table, weight_in, weight_out, scales, asked, turned_in, turned_out, owned, *ahead):
    device = lax.axis_index("dp")
    owned[0] = owner_table[device]
    owned[1] = owner_table[lax.min(device + 1 - 2 * lax.rem(device, 2), owner_table.shape[0] - 1)]
    for ref, turned in ((weight_in, turned_in), (weight_out, turned_out)):
        for rows in tiles(ref.shape[0]):
            for cols in tiles(ref.shape[1]):
                turned[cols, rows] = ref[rows, cols].T

    @pl.when(lax.axis_index("section") == last)
    def _():
        for batch, grad_act in enumerate(ahead):
            scaled = (asked[batch].astype(F32) * scales[...]).astype(BF16)
            for cols in tiles(turned_out.shape[1]):
                grad_act[:, cols] = dot(scaled, turned_out[:, cols])


def forward_kernel(step, batch, x_ref, gain, weight_in, weight_out, scales, out, acted):
    @pl.when(lax.axis_index("section") == step)
    def _():
        x = (x_ref[...] if batch is None else x_ref[batch]).astype(F32)
        normed_bf, _, _ = normalize(x, gain[...])
        for cols in tiles(weight_in.shape[1]):
            acted[:, cols] = gelu(dot(normed_bf, weight_in[:, cols])).astype(BF16)
        for cols in tiles(x.shape[1]):
            branch = dot(acted[...], weight_out[:, cols])
            out[:, cols] = (x[:, cols] + scales[:, cols] * branch).astype(BF16)


def choose(whole, batch, place, later, chosen):
    section = lax.axis_index("section")

    @pl.when(section == place)
    def _():
        chosen[...] = whole[batch]

    for index, ref in later:
        @pl.when(section == index)
        def _():
            chosen[...] = ref[...]


def save_kernel(batch, sections, *refs):
    whole, later, refs = refs[0], refs[1:sections], refs[sections:]
    gain, weight_in, normed_bf, normed, inv_std, slope, chosen = refs
    choose(whole, batch, 0, list(enumerate(later, 1)), chosen)
    normed_bf[...], normed[...], inv_std[...] = normalize(chosen[...].astype(F32), gain[...])
    for cols in tiles(weight_in.shape[1]):
        slope[:, cols] = gelu_slope(dot(normed_bf[...], weight_in[:, cols]))


def backward_kernel(
    step, batch, gy_ref, gain, turned_in, turned_out, scales, normed_ref, inv_std, slope, *refs
):
    *ahead, out, grad_hidden = refs

    @pl.when(lax.axis_index("section") == step)
    def _():
        cotangent = (gy_ref[...] if batch is None else gy_ref[batch]).astype(F32)
        scaled = (cotangent * scales[...]).astype(BF16)
        for cols in tiles(turned_out.shape[1]):
            grad_act = ahead[0][:, cols] if ahead else dot(scaled, turned_out[:, cols])
            grad_hidden[:, cols] = (grad_act * slope[:, cols]).astype(BF16)
        grad_normed = dot(grad_hidden[...], turned_in[...]) * gain[...]
        normed = normed_ref[...]
        mean_one = jnp.mean(grad_normed, axis=-1, keepdims=True)
        mean_two = jnp.mean(grad_normed * normed, axis=-1, keepdims=True)
        out[...] = (
            cotangent + inv_std[...] * (grad_normed - mean_one - normed * mean_two)
        ).astype(BF16)


def pick_kernel(batch, sections, *refs):
    whole, later, chosen = refs[0], refs[1:sections], refs[-1]
    choose(whole, batch, sections - 1, list(enumerate(later)), chosen)


def take_slopes(section, count, *refs):
    batches = (len(refs) - count - 1) // 2
    blocks, weight_in, known, slopes = refs[:count], refs[count], refs[count + 1 : -batches], refs[-batches:]
    part = known[0].shape[0]

    @pl.when(section(lax.axis_index("section")))
    def _():
        size = (count - 1) * part
        others = [block[batch * part : (batch + 1) * part, :] for batch in range(batches) for block in blocks[1:]]
        others = jnp.concatenate(others, axis=0)
        for cols in tiles(weight_in.shape[1], 256):
            values = gelu_slope(dot(others, weight_in[:, cols]))
            for batch, slope in enumerate(slopes):
                slope[part:, cols] = values[batch * size : (batch + 1) * size, :]
        for batch, slope in enumerate(slopes):
            slope[:part, :] = known[batch][...]


def slopes_kernel(count, batches, late, owned, *refs):
    sums, slopes, rows = refs[count + 1 + batches :][:2], refs[-1 - batches : -1], refs[-1]
    take_slopes(lambda section: section != late, count, *refs[: count + 1 + batches], *slopes)
    blocks = refs[:count]
    height = blocks[0].shape[0]
    for index, block in enumerate(blocks):
        rows[index * height : (index + 1) * height, :] = block[...]
    for which, total in enumerate(sums):
        for cols, value in products([rows], owned[which], total.shape[0], tiles(total.shape[1])):
            total[:, cols] = value


def late_kernel(count, batches, late, *refs):
    take_slopes(lambda section: section == late, count, *refs[: count + 1 + batches], *refs[-batches:])


def arrived_kernel(*refs):
    pass


def stack_kernel(*refs):
    *blocks, whole = refs
    height = blocks[0].shape[0]
    for index, block in enumerate(blocks):
        whole[index * height : (index + 1) * height, :] = block[...]


def hidden_kernel(places, *refs):
    count = len(places)
    blocks, (scales, turned_out, slope, grad_hidden, scaled) = refs[:count], refs[count:]
    part = blocks[0].shape[0]
    for index, block in enumerate(blocks):
        scaled[index * part : (index + 1) * part, :] = (
            block[...].astype(F32) * scales[...]
        ).astype(BF16)
    for cols in tiles(turned_out.shape[1], 256):
        grad_act = dot(scaled[...], turned_out[:, cols])
        for index, place in enumerate(places):
            rows = slice(index * part, (index + 1) * part)
            there = slope[place * part : (place + 1) * part, cols]
            grad_hidden[rows, cols] = (grad_act[rows, :] * there).astype(BF16)


def products(blocks, owner, tall, pieces, earlier=None):
    mine = pl.ds(pl.multiple_of(owner * tall, tall), tall)
    for cols in pieces:
        own = jnp.concatenate([block[:, mine] for block in blocks], axis=0)
        value = dot_tn(own, jnp.concatenate([block[:, cols] for block in blocks], axis=0))
        yield cols, value if earlier is None else earlier[:, cols] + value


def square_kernel(count, factor, owned, *refs):
    blocks, (earlier, total, stage, left) = refs[:count], refs[count:]
    tall, width = stage.shape
    copies = []
    for cols, value in products(blocks, owned[0], tall, tiles(width), earlier):
        stage[:, cols] = value * factor
        copies.append(pltpu.make_async_copy(stage.at[:, cols], total.at[:, cols], left.at[len(copies)]))
        copies[-1].start()
    for copy in copies:
        copy.wait()


def partial_kernel(count, factor, owned, *refs):
    blocks, (mine, other, total, act_share, stage, left) = refs[:count], refs[count:]
    stage[...] = (mine[...] + other[...]) * factor
    copy = pltpu.make_async_copy(stage, act_share, left.at[0])
    copy.start()
    for cols, value in products(blocks, owned[0], total.shape[0], tiles(total.shape[1])):
        total[:, cols] = value
    copy.wait()


def pinned(value):
    return pltpu.with_memory_space_constraint(value, pltpu.VMEM)


def shape(dims, dtype=BF16):
    return jax.ShapeDtypeStruct(dims, dtype)


class Order:
    def __init__(self):
        self.token = []

    def __call__(
        self, kernel, arrays, outs, scratch=(), flops=0, specs=None, name=None, aliases=None, out_specs=None, ordered=True, free=False
    ):
        count, before = len(arrays), [] if free else self.token

        def body(*refs):
            given, rest = refs[:count], refs[count + len(before) :]
            kernel(*given, *rest[: len(outs)], *rest[len(outs) + ordered :])

        results = pl.pallas_call(
            body,
            in_specs=(specs or [IN_VMEM] * count) + [IN_VMEM] * len(before),
            out_specs=(out_specs or [IN_VMEM] * len(outs)) + [IN_VMEM] * ordered,
            out_shape=[*outs] + [pltpu.VMEM((8, 128), F32)] * ordered,
            scratch_shapes=list(scratch),
            input_output_aliases=aliases or {},
            compiler_params=pltpu.CompilerParams(vmem_limit_bytes=ROOM),
            cost_estimate=pl.CostEstimate(flops=flops, bytes_accessed=8 * MIB, transcendentals=0),
            name=name,
        )(*arrays, *before)
        if ordered:
            self.token = [pinned(results[-1])]
            return results[:-1]
        return results


def stack(call, blocks):
    height, width = blocks[0].shape
    outs = [shape((height * len(blocks), width), blocks[0].dtype)]
    return call(stack_kernel, [pinned(block) for block in blocks], outs, name="stack", ordered=False, free=True)[0]


def owned_partial(call, blocks, owned, owners, factor, act_parts):
    width = blocks[0].shape[1]
    act = shape(act_parts[0].shape, F32)
    return call(
        functools.partial(partial_kernel, len(blocks), factor),
        [owned, *[pinned(value) for value in [*blocks, *act_parts]]],
        [shape((width // owners, width), F32), act],
        [pltpu.VMEM(act.shape, F32), pltpu.SemaphoreType.DMA((1,))],
        specs=[IN_SMEM] + [IN_VMEM] * (len(blocks) + 2),
        name="partial",
        out_specs=[IN_VMEM, pl.BlockSpec(memory_space=pltpu.HBM)],
        ordered=False,
    )


def owned_square(call, blocks, owned, owners, factor, earlier):
    width = blocks[0].shape[1]
    tall = width // owners
    return call(
        functools.partial(square_kernel, len(blocks), factor),
        [owned, *[pinned(value) for value in [*blocks, earlier]]],
        [shape((tall, width), F32)],
        [pltpu.VMEM((tall, width), F32), pltpu.SemaphoreType.DMA((len(tiles(width, 256)),))],
        specs=[IN_SMEM] + [IN_VMEM] * (len(blocks) + 1),
        name="square",
        out_specs=[pl.BlockSpec(memory_space=pltpu.HBM)],
        ordered=False,
    )[0]


def plain_square(rows, owner_table, owners, total_rows):
    everything = lax.all_gather(rows, "dp", axis=0, tiled=True)
    tall = rows.shape[1] // owners
    start = owner_table[lax.axis_index("dp")] * tall
    own = lax.dynamic_slice_in_dim(everything, start, tall, axis=1)
    return dot_tn(own, everything) / total_rows


def body(inputs, ln_gain, w_in, w_out, layer_scale, out_grad, owner_table):
    sections = lax.axis_size("section")
    owners = lax.axis_size("dp")
    batch_count, row_count, width = inputs.shape
    width_hidden = w_in.shape[2]
    total_rows = batch_count * row_count * owners
    batches = range(batch_count)
    product = 2 * row_count * width * width_hidden
    block = shape((row_count, width))
    wide = pltpu.VMEM((row_count, width_hidden), BF16)
    flat = pltpu.VMEM((row_count, width), BF16)
    far = [ln_gain, inputs, w_in, w_out, layer_scale, out_grad]
    sizes = [ln_gain.shape, inputs.shape, w_in.shape[1:], w_out.shape[1:], ln_gain.shape, inputs.shape]
    homes = [pltpu.VMEM(size, value.dtype) for size, value in zip(sizes, far)]
    far = [pltpu.with_memory_space_constraint(value, pltpu.HBM) for value in far]
    far_specs = [pl.BlockSpec(memory_space=pltpu.HBM)] * len(far)
    flags = pltpu.SemaphoreType.DMA((4 + 2 * len(tiles(width_hidden)),))
    call = Order()
    *near, output = call(
        first_kernel, far, homes + [block], [wide, flags], 2 * product, far_specs, "first"
    )
    arrived = [[pinned(hop(output, 0, 1))]] + [[] for m in batches[1:]]
    near = call(
        load_kernel,
        far + [pinned(value) for value in near],
        homes,
        [flags],
        specs=far_specs + [IN_VMEM] * len(near),
        name="load",
        aliases={len(far) + index: index for index in range(len(far))},
    )
    paired = owners in (2, 4, 8) and not (width // owners % 128 or width_hidden // owners % 128)
    masks = range(owners - 2, 0, -2)
    gain, given, weight_in, weight_out, scales, asked = [pinned(value) for value in near]
    for step in range(sections - 1):
        for m in batches:
            if not (step or m):
                continue
            (output,) = call(
                functools.partial(forward_kernel, step, None if step else m),
                [arrived[m][-1] if step else given, gain, weight_in, weight_out, scales],
                [block],
                [wide],
                2 * product,
                name="forward",
            )
            arrived[m].append(pinned(hop(output, step, 1)))
        if step == min(1, sections - 2):
            turned_in, turned_out, owned, *ahead = call(
                functools.partial(turn_kernel, sections - 1),
                [owner_table, weight_in, weight_out, scales, asked],
                [
                    pltpu.VMEM((width_hidden, width), BF16),
                    pltpu.VMEM((width, width_hidden), BF16),
                    pltpu.SMEM((2,), jnp.int32),
                ]
                + [shape((row_count, width_hidden), F32)] * batch_count,
                name="turn",
                specs=[IN_SMEM] + [IN_VMEM] * 4,
                out_specs=[IN_VMEM, IN_VMEM, IN_SMEM] + [IN_VMEM] * batch_count,
            )
            owned = pltpu.with_memory_space_constraint(owned, pltpu.SMEM)
            turned_in, turned_out = pinned(turned_in), pinned(turned_out)

    saved, returned = [], [[] for m in batches]
    for step in range(sections - 1, 0, -1):
        for m in batches:
            if paired and step == 1 and m == batches[-1]:
                call(arrived_kernel, [pinned(x) for x in gathered], [], name="arrived")
            if len(saved) <= m:
                values = call(
                    functools.partial(save_kernel, m, sections),
                    [given, *arrived[m], gain, weight_in],
                    [
                        block,
                        shape((row_count, width), F32),
                        shape((row_count, 1), F32),
                        shape((row_count, width_hidden), F32),
                    ],
                    [flat],
                    product,
                    name="save",
                )
                saved.append([pinned(value) for value in values])
            (grad_input,) = call(
                functools.partial(backward_kernel, step, m if step == sections - 1 else None),
                [
                    asked if step == sections - 1 else returned[m][0],
                    gain, turned_in, turned_out, scales, *saved[m][1:],
                    *([pinned(ahead[m])] if step == sections - 1 else []),
                ],
                [block],
                [wide],
                2 * product,
                name="backward",
            )
            returned[m].insert(0, pinned(hop(grad_input, step, -1)))
        if step == sections - 1:
            merged = stack(call, [saved[m][0] for m in batches])
            if paired:
                gathered = [merged] + [swapped(merged, "dp", mask) for mask in masks]
                count = len(gathered)
    factor = 1.0 / total_rows
    if paired:
        tall = width // owners
        sums = [shape((tall, width), F32)] * 2
        to_slopes = [*[pinned(x) for x in gathered], weight_in, *[saved[m][3] for m in batches]]
        own, other, *slopes = call(
            functools.partial(slopes_kernel, count, batch_count, 1),
            [owned, *to_slopes],
            [*sums, *[shape((count * row_count, width_hidden), F32)] * batch_count],
            [pltpu.VMEM((count * batch_count * row_count, width), BF16)],
            specs=[IN_SMEM] + [IN_VMEM] * (count + 1 + batch_count),
            name="slopes",
        )
        other = swapped(other, "dp", 1)
    hidden_blocks, cotangents = [], []
    for m in batches:
        (cotangent,) = call(
            functools.partial(pick_kernel, m, sections),
            [asked, *returned[m]],
            [block],
            name="pick",
            ordered=m == 0,
        )
        cotangents.append(cotangent)
        if paired and m == 0:
            slopes = call(
                functools.partial(late_kernel, count, batch_count, 1),
                [*to_slopes, *[pinned(value) for value in slopes]],
                [shape((count * row_count, width_hidden), F32)] * batch_count,
                name="late",
                aliases={len(to_slopes) + n: n for n in batches},
                )
    for m in batches:
        cotangent = cotangents[m]
        order = [mask for mask in masks if paired]
        sent = {mask: swapped(cotangent, "dp", mask) for mask in (order if m else reversed(order))}
        near = [cotangent] + [sent[mask] for mask in order]
        count = len(near)
        places = [[0, *range(3, count)], list(range(1, min(count, 3)))] if count > 1 else [[0]]
        made = [
            call(
                functools.partial(hidden_kernel, part),
                [
                    *[pinned(near[place]) for place in part],
                    scales, turned_out, pinned(slopes[m]) if paired else saved[m][3],
                ],
                [shape((len(part) * row_count, width_hidden))],
                [pltpu.VMEM((len(part) * row_count, width), BF16)],
                name="hidden",
                ordered=False,
            )[0]
            for part in places
        ]
        hidden_blocks += made
        if paired:
            crossed = [swapped(part, "dp", 1) for part in made]
            hidden_blocks += crossed
    if not paired:
        grad_rows = jnp.concatenate(hidden_blocks, axis=0)
        return (
            plain_square(merged, owner_table, owners, total_rows)[None],
            plain_square(grad_rows, owner_table, owners, total_rows)[None],
        )
    late = len(crossed)
    earlier, act_share = owned_partial(call, hidden_blocks[:-late], owned, owners, factor, [own, other])
    grad_share = owned_square(call, hidden_blocks[-late:], owned, owners, factor, earlier)
    return (act_share[None], grad_share[None])


def solution(mesh):
    placed = (
        P(None, "dp", None),
        P("section", None),
        P("section", None, None),
        P("section", None, None),
        P("section", None),
        P(None, "dp", None),
        P(),
    )
    return jax.shard_map(
        body,
        mesh=mesh,
        in_specs=placed,
        out_specs=(P("section", "dp", None), P("section", "dp", None)),
        check_vma=False,
    )
```

```python
import functools

import jax
import jax.numpy as jnp
from jax import lax
from jax.experimental import pallas as pl
from jax.experimental.pallas import tpu as pltpu
from jax.sharding import PartitionSpec as P

SQRT_HALF = 0.7071067811865476
INV_ROOT_TAU = 0.3989422804014327
F32 = jnp.float32
BF16 = jnp.bfloat16
IN_VMEM = pl.BlockSpec(memory_space=pltpu.VMEM)
IN_SMEM = pl.BlockSpec(memory_space=pltpu.SMEM)
TILE = 512
MIB = 2**20
ROOM = 24 * MIB


def hop(value, source, steps):
    return lax.ppermute(value, "section", [(source, source + steps)])


def swapped(value, axis, mask):
    count = lax.axis_size(axis)
    return lax.ppermute(value, axis, [(source, source ^ mask) for source in range(count)])


def tiles(width, most=TILE):
    size = min(most, width)
    return [slice(start, min(start + size, width)) for start in range(0, width, size)]


def dot(left, right):
    return jnp.dot(left, right, preferred_element_type=F32)


def dot_tn(left, right):
    return lax.dot_general(left, right, (((0,), (0,)), ((), ())), preferred_element_type=F32)


def normalize(floats, gain_row):
    center = floats - jnp.mean(floats, axis=-1, keepdims=True)
    inv_std = lax.rsqrt(jnp.mean(center * center, axis=-1, keepdims=True) + 1e-06)
    normed = center * inv_std
    return ((normed * gain_row).astype(BF16), normed, inv_std)


def gelu(v):
    return 0.5 * v * (1.0 + lax.erf(v * SQRT_HALF))


def gelu_slope(v):
    return 0.5 * (1.0 + lax.erf(v * SQRT_HALF)) + v * INV_ROOT_TAU * jnp.exp(-0.5 * v * v)


def arrivals(far, near, arrived):
    gain, x_all, weight_in, weight_out, scales, asked = near
    pairs = [(far[0], gain), (far[1], x_all)]
    pairs += [(far[2].at[0, :, cols], weight_in.at[:, cols]) for cols in tiles(weight_in.shape[1])]
    pairs += [(far[3].at[0, rows, :], weight_out.at[rows, :]) for rows in tiles(weight_out.shape[0])]
    pairs += [(far[4], scales), (far[5], asked)]
    return [
        pltpu.make_async_copy(source, target, arrived.at[index])
        for index, (source, target) in enumerate(pairs)
    ]


def first_kernel(*refs):
    far, near, (out, acted, arrived) = refs[:6], refs[6:12], refs[12:]
    gain, x_all, weight_in, weight_out, scales, _ = near

    @pl.when(lax.axis_index("section") == 0)
    def _():
        copies = arrivals(far, near, arrived)[:-1]
        for copy in copies:
            copy.start()
        copies[0].wait()
        copies[1].wait()
        x = x_all[0].astype(F32)
        normed_bf, _, _ = normalize(x, gain[...])
        in_tiles = tiles(weight_in.shape[1])
        for copy, cols in zip(copies[2:], in_tiles):
            copy.wait()
            acted[:, cols] = gelu(dot(normed_bf, weight_in[:, cols])).astype(BF16)
        branch = None
        for copy, rows in zip(copies[2 + len(in_tiles) :], tiles(weight_out.shape[0])):
            copy.wait()
            term = dot(acted[:, rows], weight_out[rows, :])
            branch = term if branch is None else branch + term
        copies[-1].wait()
        out[...] = (x + scales[...] * branch).astype(BF16)


def load_kernel(*refs):
    far, near, arrived = refs[:6], refs[12:18], refs[18]

    @pl.when(lax.axis_index("section") != 0)
    def _():
        copies = arrivals(far, near, arrived)
        for copy in copies:
            copy.start()
        for copy in copies:
            copy.wait()


def turn_kernel(last, owner_table, weight_in, weight_out, scales, asked, turned_in, turned_out, owned, *ahead):
    device = lax.axis_index("dp")
    owned[0] = owner_table[device]
    owned[1] = owner_table[lax.min(device + 1 - 2 * lax.rem(device, 2), owner_table.shape[0] - 1)]
    for ref, turned in ((weight_in, turned_in), (weight_out, turned_out)):
        for rows in tiles(ref.shape[0]):
            for cols in tiles(ref.shape[1]):
                turned[cols, rows] = ref[rows, cols].T

    @pl.when(lax.axis_index("section") == last)
    def _():
        for batch, grad_act in enumerate(ahead):
            scaled = (asked[batch].astype(F32) * scales[...]).astype(BF16)
            for cols in tiles(turned_out.shape[1]):
                grad_act[:, cols] = dot(scaled, turned_out[:, cols])


def forward_kernel(step, batch, x_ref, gain, weight_in, weight_out, scales, out, acted):
    @pl.when(lax.axis_index("section") == step)
    def _():
        x = (x_ref[...] if batch is None else x_ref[batch]).astype(F32)
        normed_bf, _, _ = normalize(x, gain[...])
        for cols in tiles(weight_in.shape[1]):
            acted[:, cols] = gelu(dot(normed_bf, weight_in[:, cols])).astype(BF16)
        for cols in tiles(x.shape[1]):
            branch = dot(acted[...], weight_out[:, cols])
            out[:, cols] = (x[:, cols] + scales[:, cols] * branch).astype(BF16)


def choose(whole, batch, place, later, chosen):
    section = lax.axis_index("section")

    @pl.when(section == place)
    def _():
        chosen[...] = whole[batch]

    for index, ref in later:
        @pl.when(section == index)
        def _():
            chosen[...] = ref[...]


def save_kernel(batch, sections, *refs):
    whole, later, refs = refs[0], refs[1:sections], refs[sections:]
    gain, weight_in, normed_bf, normed, inv_std, slope, chosen = refs
    choose(whole, batch, 0, list(enumerate(later, 1)), chosen)
    normed_bf[...], normed[...], inv_std[...] = normalize(chosen[...].astype(F32), gain[...])
    for cols in tiles(weight_in.shape[1]):
        slope[:, cols] = gelu_slope(dot(normed_bf[...], weight_in[:, cols]))


def backward_kernel(
    step, batch, gy_ref, gain, turned_in, turned_out, scales, normed_ref, inv_std, slope, *refs
):
    *ahead, out, grad_hidden = refs

    @pl.when(lax.axis_index("section") == step)
    def _():
        cotangent = (gy_ref[...] if batch is None else gy_ref[batch]).astype(F32)
        scaled = (cotangent * scales[...]).astype(BF16)
        for cols in tiles(turned_out.shape[1]):
            grad_act = ahead[0][:, cols] if ahead else dot(scaled, turned_out[:, cols])
            grad_hidden[:, cols] = (grad_act * slope[:, cols]).astype(BF16)
        grad_normed = dot(grad_hidden[...], turned_in[...]) * gain[...]
        normed = normed_ref[...]
        mean_one = jnp.mean(grad_normed, axis=-1, keepdims=True)
        mean_two = jnp.mean(grad_normed * normed, axis=-1, keepdims=True)
        out[...] = (
            cotangent + inv_std[...] * (grad_normed - mean_one - normed * mean_two)
        ).astype(BF16)


def pick_kernel(batch, sections, *refs):
    whole, later, chosen = refs[0], refs[1:sections], refs[-1]
    choose(whole, batch, sections - 1, list(enumerate(later)), chosen)


def take_slopes(section, count, *refs):
    batches = (len(refs) - count - 1) // 2
    blocks, weight_in, known, slopes = refs[:count], refs[count], refs[count + 1 : -batches], refs[-batches:]
    part = known[0].shape[0]

    @pl.when(section(lax.axis_index("section")))
    def _():
        size = (count - 1) * part
        others = [block[batch * part : (batch + 1) * part, :] for batch in range(batches) for block in blocks[1:]]
        others = jnp.concatenate(others, axis=0)
        for cols in tiles(weight_in.shape[1], 256):
            values = gelu_slope(dot(others, weight_in[:, cols]))
            for batch, slope in enumerate(slopes):
                slope[part:, cols] = values[batch * size : (batch + 1) * size, :]
        for batch, slope in enumerate(slopes):
            slope[:part, :] = known[batch][...]


def slopes_kernel(count, batches, late, owned, *refs):
    sums, slopes, rows = refs[count + 1 + batches :][:2], refs[-1 - batches : -1], refs[-1]
    take_slopes(lambda section: section != late, count, *refs[: count + 1 + batches], *slopes)
    blocks = refs[:count]
    height = blocks[0].shape[0]
    for index, block in enumerate(blocks):
        rows[index * height : (index + 1) * height, :] = block[...]
    for which, total in enumerate(sums):
        for cols, value in products([rows], owned[which], total.shape[0], tiles(total.shape[1])):
            total[:, cols] = value


def late_kernel(count, batches, late, *refs):
    take_slopes(lambda section: section == late, count, *refs[: count + 1 + batches], *refs[-batches:])


def arrived_kernel(*refs):
    pass


def stack_kernel(*refs):
    *blocks, whole = refs
    height = blocks[0].shape[0]
    for index, block in enumerate(blocks):
        whole[index * height : (index + 1) * height, :] = block[...]


def hidden_kernel(places, *refs):
    count = len(places)
    blocks, (scales, turned_out, slope, grad_hidden, scaled) = refs[:count], refs[count:]
    part = blocks[0].shape[0]
    for index, block in enumerate(blocks):
        scaled[index * part : (index + 1) * part, :] = (
            block[...].astype(F32) * scales[...]
        ).astype(BF16)
    for cols in tiles(turned_out.shape[1], 256):
        grad_act = dot(scaled[...], turned_out[:, cols])
        for index, place in enumerate(places):
            rows = slice(index * part, (index + 1) * part)
            there = slope[place * part : (place + 1) * part, cols]
            grad_hidden[rows, cols] = (grad_act[rows, :] * there).astype(BF16)


def products(blocks, owner, tall, pieces, earlier=None):
    mine = pl.ds(pl.multiple_of(owner * tall, tall), tall)
    for cols in pieces:
        own = jnp.concatenate([block[:, mine] for block in blocks], axis=0)
        value = dot_tn(own, jnp.concatenate([block[:, cols] for block in blocks], axis=0))
        yield cols, value if earlier is None else earlier[:, cols] + value


def square_kernel(count, factor, owned, *refs):
    blocks, (earlier, total, stage, left) = refs[:count], refs[count:]
    tall, width = stage.shape
    copies = []
    for cols, value in products(blocks, owned[0], tall, tiles(width), earlier):
        stage[:, cols] = value * factor
        copies.append(pltpu.make_async_copy(stage.at[:, cols], total.at[:, cols], left.at[len(copies)]))
        copies[-1].start()
    for copy in copies:
        copy.wait()


def partial_kernel(count, factor, owned, *refs):
    blocks, (mine, other, total, act_share, stage, left) = refs[:count], refs[count:]
    stage[...] = (mine[...] + other[...]) * factor
    copy = pltpu.make_async_copy(stage, act_share, left.at[0])
    copy.start()
    for cols, value in products(blocks, owned[0], total.shape[0], tiles(total.shape[1])):
        total[:, cols] = value
    copy.wait()


def pinned(value):
    return pltpu.with_memory_space_constraint(value, pltpu.VMEM)


def shape(dims, dtype=BF16):
    return jax.ShapeDtypeStruct(dims, dtype)


class Order:
    def __init__(self):
        self.token = []

    def __call__(
        self, kernel, arrays, outs, scratch=(), flops=0, specs=None, name=None, aliases=None, out_specs=None, ordered=True, free=False
    ):
        count, before = len(arrays), [] if free else self.token

        def body(*refs):
            given, rest = refs[:count], refs[count + len(before) :]
            kernel(*given, *rest[: len(outs)], *rest[len(outs) + ordered :])

        results = pl.pallas_call(
            body,
            in_specs=(specs or [IN_VMEM] * count) + [IN_VMEM] * len(before),
            out_specs=(out_specs or [IN_VMEM] * len(outs)) + [IN_VMEM] * ordered,
            out_shape=[*outs] + [pltpu.VMEM((8, 128), F32)] * ordered,
            scratch_shapes=list(scratch),
            input_output_aliases=aliases or {},
            compiler_params=pltpu.CompilerParams(vmem_limit_bytes=ROOM),
            cost_estimate=pl.CostEstimate(flops=flops, bytes_accessed=8 * MIB, transcendentals=0),
            name=name,
        )(*arrays, *before)
        if ordered:
            self.token = [pinned(results[-1])]
            return results[:-1]
        return results


def stack(call, blocks):
    height, width = blocks[0].shape
    outs = [shape((height * len(blocks), width), blocks[0].dtype)]
    return call(stack_kernel, [pinned(block) for block in blocks], outs, name="stack", ordered=False, free=True)[0]


def owned_partial(call, blocks, owned, owners, factor, act_parts):
    width = blocks[0].shape[1]
    act = shape(act_parts[0].shape, F32)
    return call(
        functools.partial(partial_kernel, len(blocks), factor),
        [owned, *[pinned(value) for value in [*blocks, *act_parts]]],
        [shape((width // owners, width), F32), act],
        [pltpu.VMEM(act.shape, F32), pltpu.SemaphoreType.DMA((1,))],
        specs=[IN_SMEM] + [IN_VMEM] * (len(blocks) + 2),
        name="partial",
        out_specs=[IN_VMEM, pl.BlockSpec(memory_space=pltpu.HBM)],
        ordered=False,
    )


def owned_square(call, blocks, owned, owners, factor, earlier):
    width = blocks[0].shape[1]
    tall = width // owners
    return call(
        functools.partial(square_kernel, len(blocks), factor),
        [owned, *[pinned(value) for value in [*blocks, earlier]]],
        [shape((tall, width), F32)],
        [pltpu.VMEM((tall, width), F32), pltpu.SemaphoreType.DMA((len(tiles(width, 256)),))],
        specs=[IN_SMEM] + [IN_VMEM] * (len(blocks) + 1),
        name="square",
        out_specs=[pl.BlockSpec(memory_space=pltpu.HBM)],
        ordered=False,
    )[0]


def plain_square(rows, owner_table, owners, total_rows):
    everything = lax.all_gather(rows, "dp", axis=0, tiled=True)
    tall = rows.shape[1] // owners
    start = owner_table[lax.axis_index("dp")] * tall
    own = lax.dynamic_slice_in_dim(everything, start, tall, axis=1)
    return dot_tn(own, everything) / total_rows


def body(inputs, ln_gain, w_in, w_out, layer_scale, out_grad, owner_table):
    sections = lax.axis_size("section")
    owners = lax.axis_size("dp")
    batch_count, row_count, width = inputs.shape
    width_hidden = w_in.shape[2]
    total_rows = batch_count * row_count * owners
    batches = range(batch_count)
    product = 2 * row_count * width * width_hidden
    block = shape((row_count, width))
    wide = pltpu.VMEM((row_count, width_hidden), BF16)
    flat = pltpu.VMEM((row_count, width), BF16)
    far = [ln_gain, inputs, w_in, w_out, layer_scale, out_grad]
    sizes = [ln_gain.shape, inputs.shape, w_in.shape[1:], w_out.shape[1:], ln_gain.shape, inputs.shape]
    homes = [pltpu.VMEM(size, value.dtype) for size, value in zip(sizes, far)]
    far = [pltpu.with_memory_space_constraint(value, pltpu.HBM) for value in far]
    far_specs = [pl.BlockSpec(memory_space=pltpu.HBM)] * len(far)
    flags = pltpu.SemaphoreType.DMA((4 + 2 * len(tiles(width_hidden)),))
    call = Order()
    *near, output = call(
        first_kernel, far, homes + [block], [wide, flags], 2 * product, far_specs, "first"
    )
    arrived = [[pinned(hop(output, 0, 1))]] + [[] for m in batches[1:]]
    near = call(
        load_kernel,
        far + [pinned(value) for value in near],
        homes,
        [flags],
        specs=far_specs + [IN_VMEM] * len(near),
        name="load",
        aliases={len(far) + index: index for index in range(len(far))},
    )
    paired = owners in (2, 4, 8) and not (width // owners % 128 or width_hidden // owners % 128)
    masks = range(owners - 2, 0, -2)
    gain, given, weight_in, weight_out, scales, asked = [pinned(value) for value in near]
    for step in range(sections - 1):
        for m in batches:
            if not (step or m):
                continue
            (output,) = call(
                functools.partial(forward_kernel, step, None if step else m),
                [arrived[m][-1] if step else given, gain, weight_in, weight_out, scales],
                [block],
                [wide],
                2 * product,
                name="forward",
            )
            arrived[m].append(pinned(hop(output, step, 1)))
        if step == min(1, sections - 2):
            turned_in, turned_out, owned, *ahead = call(
                functools.partial(turn_kernel, sections - 1),
                [owner_table, weight_in, weight_out, scales, asked],
                [
                    pltpu.VMEM((width_hidden, width), BF16),
                    pltpu.VMEM((width, width_hidden), BF16),
                    pltpu.SMEM((2,), jnp.int32),
                ]
                + [shape((row_count, width_hidden), F32)] * batch_count,
                name="turn",
                specs=[IN_SMEM] + [IN_VMEM] * 4,
                out_specs=[IN_VMEM, IN_VMEM, IN_SMEM] + [IN_VMEM] * batch_count,
            )
            owned = pltpu.with_memory_space_constraint(owned, pltpu.SMEM)
            turned_in, turned_out = pinned(turned_in), pinned(turned_out)

    saved, returned = [], [[] for m in batches]
    for step in range(sections - 1, 0, -1):
        for m in batches:
            if paired and step == 1 and m == batches[-1]:
                call(arrived_kernel, [pinned(x) for x in gathered], [], name="arrived")
            if len(saved) <= m:
                values = call(
                    functools.partial(save_kernel, m, sections),
                    [given, *arrived[m], gain, weight_in],
                    [
                        block,
                        shape((row_count, width), F32),
                        shape((row_count, 1), F32),
                        shape((row_count, width_hidden), F32),
                    ],
                    [flat],
                    product,
                    name="save",
                )
                saved.append([pinned(value) for value in values])
            (grad_input,) = call(
                functools.partial(backward_kernel, step, m if step == sections - 1 else None),
                [
                    asked if step == sections - 1 else returned[m][0],
                    gain, turned_in, turned_out, scales, *saved[m][1:],
                    *([pinned(ahead[m])] if step == sections - 1 else []),
                ],
                [block],
                [wide],
                2 * product,
                name="backward",
            )
            returned[m].insert(0, pinned(hop(grad_input, step, -1)))
        if step == sections - 1:
            merged = stack(call, [saved[m][0] for m in batches])
            if paired:
                gathered = [merged] + [swapped(merged, "dp", mask) for mask in masks]
                count = len(gathered)
    factor = 1.0 / total_rows
    if paired:
        tall = width // owners
        sums = [shape((tall, width), F32)] * 2
        to_slopes = [*[pinned(x) for x in gathered], weight_in, *[saved[m][3] for m in batches]]
        own, other, *slopes = call(
            functools.partial(slopes_kernel, count, batch_count, 1),
            [owned, *to_slopes],
            [*sums, *[shape((count * row_count, width_hidden), F32)] * batch_count],
            [pltpu.VMEM((count * batch_count * row_count, width), BF16)],
            specs=[IN_SMEM] + [IN_VMEM] * (count + 1 + batch_count),
            name="slopes",
        )
        other = swapped(other, "dp", 1)
    hidden_blocks, cotangents = [], []
    for m in batches:
        (cotangent,) = call(
            functools.partial(pick_kernel, m, sections),
            [asked, *returned[m]],
            [block],
            name="pick",
            ordered=m == 0,
        )
        cotangents.append(cotangent)
        if paired and m == 0:
            slopes = call(
                functools.partial(late_kernel, count, batch_count, 1),
                [*to_slopes, *[pinned(value) for value in slopes]],
                [shape((count * row_count, width_hidden), F32)] * batch_count,
                name="late",
                aliases={len(to_slopes) + n: n for n in batches},
                )
    for m in batches:
        cotangent = cotangents[m]
        order = [mask for mask in masks if paired]
        sent = {mask: swapped(cotangent, "dp", mask) for mask in (order if m else reversed(order))}
        near = [cotangent] + [sent[mask] for mask in order]
        count = len(near)
        places = [[0, *range(3, count)], list(range(1, min(count, 3)))] if count > 1 else [[0]]
        made = [
            call(
                functools.partial(hidden_kernel, part),
                [
                    *[pinned(near[place]) for place in part],
                    scales, turned_out, pinned(slopes[m]) if paired else saved[m][3],
                ],
                [shape((len(part) * row_count, width_hidden))],
                [pltpu.VMEM((len(part) * row_count, width), BF16)],
                name="hidden",
                ordered=False,
            )[0]
            for part in places
        ]
        hidden_blocks += made
        if paired:
            crossed = [swapped(part, "dp", 1) for part in made]
            hidden_blocks += crossed
    if not paired:
        grad_rows = jnp.concatenate(hidden_blocks, axis=0)
        return (
            plain_square(merged, owner_table, owners, total_rows)[None],
            plain_square(grad_rows, owner_table, owners, total_rows)[None],
        )
    late = len(crossed)
    earlier, act_share = owned_partial(call, hidden_blocks[:-late], owned, owners, factor, [own, other])
    grad_share = owned_square(call, hidden_blocks[-late:], owned, owners, factor, earlier)
    return (act_share[None], grad_share[None])


def solution(mesh):
    placed = (
        P(None, "dp", None),
        P("section", None),
        P("section", None, None),
        P("section", None, None),
        P("section", None),
        P(None, "dp", None),
        P(),
    )
    return jax.shard_map(
        body,
        mesh=mesh,
        in_specs=placed,
        out_specs=(P("section", "dp", None), P("section", "dp", None)),
        check_vma=False,
    )
```

```python
import functools

import jax
import jax.numpy as jnp
from jax import lax
from jax.experimental import pallas as pl
from jax.experimental.pallas import tpu as pltpu
from jax.sharding import PartitionSpec as P

SQRT_HALF = 0.7071067811865476
INV_ROOT_TAU = 0.3989422804014327
F32 = jnp.float32
BF16 = jnp.bfloat16
IN_VMEM = pl.BlockSpec(memory_space=pltpu.VMEM)
IN_SMEM = pl.BlockSpec(memory_space=pltpu.SMEM)
TILE = 512
MIB = 2**20
ROOM = 24 * MIB


def hop(value, source, steps):
    return lax.ppermute(value, "section", [(source, source + steps)])


def swapped(value, axis, mask):
    count = lax.axis_size(axis)
    return lax.ppermute(value, axis, [(source, source ^ mask) for source in range(count)])


def tiles(width, most=TILE):
    size = min(most, width)
    return [slice(start, min(start + size, width)) for start in range(0, width, size)]


def dot(left, right):
    return jnp.dot(left, right, preferred_element_type=F32)


def dot_tn(left, right):
    return lax.dot_general(left, right, (((0,), (0,)), ((), ())), preferred_element_type=F32)


def normalize(floats, gain_row):
    center = floats - jnp.mean(floats, axis=-1, keepdims=True)
    inv_std = lax.rsqrt(jnp.mean(center * center, axis=-1, keepdims=True) + 1e-06)
    normed = center * inv_std
    return ((normed * gain_row).astype(BF16), normed, inv_std)


def gelu(v):
    return 0.5 * v * (1.0 + lax.erf(v * SQRT_HALF))


def gelu_slope(v):
    return 0.5 * (1.0 + lax.erf(v * SQRT_HALF)) + v * INV_ROOT_TAU * jnp.exp(-0.5 * v * v)


def arrivals(far, near, arrived):
    gain, x_all, weight_in, weight_out, scales, asked = near
    pairs = [(far[0], gain), (far[1], x_all)]
    pairs += [(far[2].at[0, :, cols], weight_in.at[:, cols]) for cols in tiles(weight_in.shape[1])]
    pairs += [(far[3].at[0, rows, :], weight_out.at[rows, :]) for rows in tiles(weight_out.shape[0])]
    pairs += [(far[4], scales), (far[5], asked)]
    return [
        pltpu.make_async_copy(source, target, arrived.at[index])
        for index, (source, target) in enumerate(pairs)
    ]


def first_kernel(*refs):
    far, near, (out, acted, arrived) = refs[:6], refs[6:12], refs[12:]
    gain, x_all, weight_in, weight_out, scales, _ = near

    @pl.when(lax.axis_index("section") == 0)
    def _():
        copies = arrivals(far, near, arrived)[:-1]
        for copy in copies:
            copy.start()
        copies[0].wait()
        copies[1].wait()
        x = x_all[0].astype(F32)
        normed_bf, _, _ = normalize(x, gain[...])
        in_tiles = tiles(weight_in.shape[1])
        for copy, cols in zip(copies[2:], in_tiles):
            copy.wait()
            acted[:, cols] = gelu(dot(normed_bf, weight_in[:, cols])).astype(BF16)
        branch = None
        for copy, rows in zip(copies[2 + len(in_tiles) :], tiles(weight_out.shape[0])):
            copy.wait()
            term = dot(acted[:, rows], weight_out[rows, :])
            branch = term if branch is None else branch + term
        copies[-1].wait()
        out[...] = (x + scales[...] * branch).astype(BF16)


def load_kernel(*refs):
    far, near, arrived = refs[:6], refs[12:18], refs[18]

    @pl.when(lax.axis_index("section") != 0)
    def _():
        copies = arrivals(far, near, arrived)
        for copy in copies:
            copy.start()
        for copy in copies:
            copy.wait()


def turn_kernel(last, owner_table, weight_in, weight_out, scales, asked, turned_in, turned_out, owned, *ahead):
    device = lax.axis_index("dp")
    owned[0] = owner_table[device]
    owned[1] = owner_table[lax.min(device + 1 - 2 * lax.rem(device, 2), owner_table.shape[0] - 1)]
    for ref, turned in ((weight_in, turned_in), (weight_out, turned_out)):
        for rows in tiles(ref.shape[0]):
            for cols in tiles(ref.shape[1]):
                turned[cols, rows] = ref[rows, cols].T

    @pl.when(lax.axis_index("section") == last)
    def _():
        for batch, grad_act in enumerate(ahead):
            scaled = (asked[batch].astype(F32) * scales[...]).astype(BF16)
            for cols in tiles(turned_out.shape[1]):
                grad_act[:, cols] = dot(scaled, turned_out[:, cols])


def forward_kernel(step, batch, x_ref, gain, weight_in, weight_out, scales, out, acted):
    @pl.when(lax.axis_index("section") == step)
    def _():
        x = (x_ref[...] if batch is None else x_ref[batch]).astype(F32)
        normed_bf, _, _ = normalize(x, gain[...])
        for cols in tiles(weight_in.shape[1]):
            acted[:, cols] = gelu(dot(normed_bf, weight_in[:, cols])).astype(BF16)
        for cols in tiles(x.shape[1]):
            branch = dot(acted[...], weight_out[:, cols])
            out[:, cols] = (x[:, cols] + scales[:, cols] * branch).astype(BF16)


def choose(whole, batch, place, later, chosen):
    section = lax.axis_index("section")

    @pl.when(section == place)
    def _():
        chosen[...] = whole[batch]

    for index, ref in later:
        @pl.when(section == index)
        def _():
            chosen[...] = ref[...]


def save_kernel(batch, sections, *refs):
    whole, later, refs = refs[0], refs[1:sections], refs[sections:]
    gain, weight_in, normed_bf, normed, inv_std, slope, chosen = refs
    choose(whole, batch, 0, list(enumerate(later, 1)), chosen)
    normed_bf[...], normed[...], inv_std[...] = normalize(chosen[...].astype(F32), gain[...])
    for cols in tiles(weight_in.shape[1]):
        slope[:, cols] = gelu_slope(dot(normed_bf[...], weight_in[:, cols]))


def backward_kernel(
    step, batch, gy_ref, gain, turned_in, turned_out, scales, normed_ref, inv_std, slope, *refs
):
    *ahead, out, grad_hidden = refs

    @pl.when(lax.axis_index("section") == step)
    def _():
        cotangent = (gy_ref[...] if batch is None else gy_ref[batch]).astype(F32)
        scaled = (cotangent * scales[...]).astype(BF16)
        for cols in tiles(turned_out.shape[1]):
            grad_act = ahead[0][:, cols] if ahead else dot(scaled, turned_out[:, cols])
            grad_hidden[:, cols] = (grad_act * slope[:, cols]).astype(BF16)
        grad_normed = dot(grad_hidden[...], turned_in[...]) * gain[...]
        normed = normed_ref[...]
        mean_one = jnp.mean(grad_normed, axis=-1, keepdims=True)
        mean_two = jnp.mean(grad_normed * normed, axis=-1, keepdims=True)
        out[...] = (
            cotangent + inv_std[...] * (grad_normed - mean_one - normed * mean_two)
        ).astype(BF16)


def pick_kernel(batch, sections, *refs):
    whole, later, chosen = refs[0], refs[1:sections], refs[-1]
    choose(whole, batch, sections - 1, list(enumerate(later)), chosen)


def take_slopes(section, count, which, *refs):
    batches = len(which)
    blocks, weight_in, known, slopes = refs[:count], refs[count], refs[count + 1 : -batches], refs[-batches:]
    part = known[0].shape[0]

    @pl.when(section(lax.axis_index("section")))
    def _():
        size = (count - 1) * part
        others = [block[batch * part : (batch + 1) * part, :] for batch in which for block in blocks[1:]]
        others = jnp.concatenate(others, axis=0)
        for cols in tiles(weight_in.shape[1], 256):
            values = gelu_slope(dot(others, weight_in[:, cols]))
            for index, slope in enumerate(slopes):
                slope[part:, cols] = values[index * size : (index + 1) * size, :]
        for index, slope in enumerate(slopes):
            slope[:part, :] = known[index][...]


def slopes_kernel(count, batches, late, owned, *refs):
    sums, slopes, rows = refs[count + 1 + batches :][:2], refs[-1 - batches : -1], refs[-1]
    take_slopes(lambda section: section != late, count, range(batches), *refs[: count + 1 + batches], *slopes)
    blocks = refs[:count]
    height = blocks[0].shape[0]
    for index, block in enumerate(blocks):
        rows[index * height : (index + 1) * height, :] = block[...]
    for which, total in enumerate(sums):
        for cols, value in products([rows], owned[which], total.shape[0], tiles(total.shape[1])):
            total[:, cols] = value


def late_kernel(count, batch, late, *refs):
    take_slopes(lambda section: section == late, count, [batch], *refs[: count + 2], refs[-1])


def arrived_kernel(*refs):
    pass


def stack_kernel(*refs):
    *blocks, whole = refs
    height = blocks[0].shape[0]
    for index, block in enumerate(blocks):
        whole[index * height : (index + 1) * height, :] = block[...]


def hidden_kernel(places, *refs):
    count = len(places)
    blocks, (scales, turned_out, slope, grad_hidden, scaled) = refs[:count], refs[count:]
    part = blocks[0].shape[0]
    for index, block in enumerate(blocks):
        scaled[index * part : (index + 1) * part, :] = (
            block[...].astype(F32) * scales[...]
        ).astype(BF16)
    for cols in tiles(turned_out.shape[1], 256):
        grad_act = dot(scaled[...], turned_out[:, cols])
        for index, place in enumerate(places):
            rows = slice(index * part, (index + 1) * part)
            there = slope[place * part : (place + 1) * part, cols]
            grad_hidden[rows, cols] = (grad_act[rows, :] * there).astype(BF16)


def products(blocks, owner, tall, pieces, earlier=None):
    mine = pl.ds(pl.multiple_of(owner * tall, tall), tall)
    for cols in pieces:
        own = jnp.concatenate([block[:, mine] for block in blocks], axis=0)
        value = dot_tn(own, jnp.concatenate([block[:, cols] for block in blocks], axis=0))
        yield cols, value if earlier is None else earlier[:, cols] + value


def square_kernel(count, factor, owned, *refs):
    blocks, (earlier, total, stage, left) = refs[:count], refs[count:]
    tall, width = stage.shape
    copies = []
    for cols, value in products(blocks, owned[0], tall, tiles(width), earlier):
        stage[:, cols] = value * factor
        copies.append(pltpu.make_async_copy(stage.at[:, cols], total.at[:, cols], left.at[len(copies)]))
        copies[-1].start()
    for copy in copies:
        copy.wait()


def partial_kernel(count, factor, owned, *refs):
    blocks, (mine, other, total, act_share, stage, left) = refs[:count], refs[count:]
    stage[...] = (mine[...] + other[...]) * factor
    copy = pltpu.make_async_copy(stage, act_share, left.at[0])
    copy.start()
    for cols, value in products(blocks, owned[0], total.shape[0], tiles(total.shape[1])):
        total[:, cols] = value
    copy.wait()


def pinned(value):
    return pltpu.with_memory_space_constraint(value, pltpu.VMEM)


def shape(dims, dtype=BF16):
    return jax.ShapeDtypeStruct(dims, dtype)


class Order:
    def __init__(self):
        self.token = []

    def __call__(
        self, kernel, arrays, outs, scratch=(), flops=0, specs=None, name=None, aliases=None, out_specs=None, ordered=True, free=False
    ):
        count, before = len(arrays), [] if free else self.token

        def body(*refs):
            given, rest = refs[:count], refs[count + len(before) :]
            kernel(*given, *rest[: len(outs)], *rest[len(outs) + ordered :])

        results = pl.pallas_call(
            body,
            in_specs=(specs or [IN_VMEM] * count) + [IN_VMEM] * len(before),
            out_specs=(out_specs or [IN_VMEM] * len(outs)) + [IN_VMEM] * ordered,
            out_shape=[*outs] + [pltpu.VMEM((8, 128), F32)] * ordered,
            scratch_shapes=list(scratch),
            input_output_aliases=aliases or {},
            compiler_params=pltpu.CompilerParams(vmem_limit_bytes=ROOM),
            cost_estimate=pl.CostEstimate(flops=flops, bytes_accessed=8 * MIB, transcendentals=0),
            name=name,
        )(*arrays, *before)
        if ordered:
            self.token = [pinned(results[-1])]
            return results[:-1]
        return results


def stack(call, blocks):
    height, width = blocks[0].shape
    outs = [shape((height * len(blocks), width), blocks[0].dtype)]
    return call(stack_kernel, [pinned(block) for block in blocks], outs, name="stack", ordered=False, free=True)[0]


def owned_partial(call, blocks, owned, owners, factor, act_parts):
    width = blocks[0].shape[1]
    act = shape(act_parts[0].shape, F32)
    return call(
        functools.partial(partial_kernel, len(blocks), factor),
        [owned, *[pinned(value) for value in [*blocks, *act_parts]]],
        [shape((width // owners, width), F32), act],
        [pltpu.VMEM(act.shape, F32), pltpu.SemaphoreType.DMA((1,))],
        specs=[IN_SMEM] + [IN_VMEM] * (len(blocks) + 2),
        name="partial",
        out_specs=[IN_VMEM, pl.BlockSpec(memory_space=pltpu.HBM)],
        ordered=False,
    )


def owned_square(call, blocks, owned, owners, factor, earlier):
    width = blocks[0].shape[1]
    tall = width // owners
    return call(
        functools.partial(square_kernel, len(blocks), factor),
        [owned, *[pinned(value) for value in [*blocks, earlier]]],
        [shape((tall, width), F32)],
        [pltpu.VMEM((tall, width), F32), pltpu.SemaphoreType.DMA((len(tiles(width, 256)),))],
        specs=[IN_SMEM] + [IN_VMEM] * (len(blocks) + 1),
        name="square",
        out_specs=[pl.BlockSpec(memory_space=pltpu.HBM)],
        ordered=False,
    )[0]


def plain_square(rows, owner_table, owners, total_rows):
    everything = lax.all_gather(rows, "dp", axis=0, tiled=True)
    tall = rows.shape[1] // owners
    start = owner_table[lax.axis_index("dp")] * tall
    own = lax.dynamic_slice_in_dim(everything, start, tall, axis=1)
    return dot_tn(own, everything) / total_rows


def body(inputs, ln_gain, w_in, w_out, layer_scale, out_grad, owner_table):
    sections = lax.axis_size("section")
    owners = lax.axis_size("dp")
    batch_count, row_count, width = inputs.shape
    width_hidden = w_in.shape[2]
    total_rows = batch_count * row_count * owners
    batches = range(batch_count)
    product = 2 * row_count * width * width_hidden
    block = shape((row_count, width))
    wide = pltpu.VMEM((row_count, width_hidden), BF16)
    flat = pltpu.VMEM((row_count, width), BF16)
    far = [ln_gain, inputs, w_in, w_out, layer_scale, out_grad]
    sizes = [ln_gain.shape, inputs.shape, w_in.shape[1:], w_out.shape[1:], ln_gain.shape, inputs.shape]
    homes = [pltpu.VMEM(size, value.dtype) for size, value in zip(sizes, far)]
    far = [pltpu.with_memory_space_constraint(value, pltpu.HBM) for value in far]
    far_specs = [pl.BlockSpec(memory_space=pltpu.HBM)] * len(far)
    flags = pltpu.SemaphoreType.DMA((4 + 2 * len(tiles(width_hidden)),))
    call = Order()
    *near, output = call(
        first_kernel, far, homes + [block], [wide, flags], 2 * product, far_specs, "first"
    )
    arrived = [[pinned(hop(output, 0, 1))]] + [[] for m in batches[1:]]
    near = call(
        load_kernel,
        far + [pinned(value) for value in near],
        homes,
        [flags],
        specs=far_specs + [IN_VMEM] * len(near),
        name="load",
        aliases={len(far) + index: index for index in range(len(far))},
    )
    paired = owners in (2, 4, 8) and not (width // owners % 128 or width_hidden // owners % 128)
    masks = range(2, owners, 2)
    gain, given, weight_in, weight_out, scales, asked = [pinned(value) for value in near]
    for step in range(sections - 1):
        for m in batches:
            if not (step or m):
                continue
            (output,) = call(
                functools.partial(forward_kernel, step, None if step else m),
                [arrived[m][-1] if step else given, gain, weight_in, weight_out, scales],
                [block],
                [wide],
                2 * product,
                name="forward",
            )
            arrived[m].append(pinned(hop(output, step, 1)))
        if step == min(1, sections - 2):
            turned_in, turned_out, owned, *ahead = call(
                functools.partial(turn_kernel, sections - 1),
                [owner_table, weight_in, weight_out, scales, asked],
                [
                    pltpu.VMEM((width_hidden, width), BF16),
                    pltpu.VMEM((width, width_hidden), BF16),
                    pltpu.SMEM((2,), jnp.int32),
                ]
                + [shape((row_count, width_hidden), F32)] * batch_count,
                name="turn",
                specs=[IN_SMEM] + [IN_VMEM] * 4,
                out_specs=[IN_VMEM, IN_VMEM, IN_SMEM] + [IN_VMEM] * batch_count,
            )
            owned = pltpu.with_memory_space_constraint(owned, pltpu.SMEM)
            turned_in, turned_out = pinned(turned_in), pinned(turned_out)

    saved, returned = [], [[] for m in batches]
    for step in range(sections - 1, 0, -1):
        for m in batches:
            if paired and step == 1 and m == batches[-1]:
                call(arrived_kernel, [pinned(x) for x in gathered], [], name="arrived")
            if len(saved) <= m:
                values = call(
                    functools.partial(save_kernel, m, sections),
                    [given, *arrived[m], gain, weight_in],
                    [
                        block,
                        shape((row_count, width), F32),
                        shape((row_count, 1), F32),
                        shape((row_count, width_hidden), F32),
                    ],
                    [flat],
                    product,
                    name="save",
                )
                saved.append([pinned(value) for value in values])
            (grad_input,) = call(
                functools.partial(backward_kernel, step, m if step == sections - 1 else None),
                [
                    asked if step == sections - 1 else returned[m][0],
                    gain, turned_in, turned_out, scales, *saved[m][1:],
                    *([pinned(ahead[m])] if step == sections - 1 else []),
                ],
                [block],
                [wide],
                2 * product,
                name="backward",
            )
            returned[m].insert(0, pinned(hop(grad_input, step, -1)))
        if step == sections - 1:
            merged = stack(call, [saved[m][0] for m in batches])
            if paired:
                gathered = [merged] + [swapped(merged, "dp", mask) for mask in masks]
                count = len(gathered)
    factor = 1.0 / total_rows
    if paired:
        tall = width // owners
        sums = [shape((tall, width), F32)] * 2
        to_slopes = [*[pinned(x) for x in gathered], weight_in, *[saved[m][3] for m in batches]]
        own, other, *slopes = call(
            functools.partial(slopes_kernel, count, batch_count, 1),
            [owned, *to_slopes],
            [*sums, *[shape((count * row_count, width_hidden), F32)] * batch_count],
            [pltpu.VMEM((count * batch_count * row_count, width), BF16)],
            specs=[IN_SMEM] + [IN_VMEM] * (count + 1 + batch_count),
            name="slopes",
        )
        other = swapped(other, "dp", 1)
    hidden_blocks, cotangents = [], []
    for m in batches:
        (cotangent,) = call(
            functools.partial(pick_kernel, m, sections),
            [asked, *returned[m]],
            [block],
            name="pick",
        )
        cotangents.append(cotangent)
        if paired:
            slopes[m] = call(
                functools.partial(late_kernel, count, m, 1),
                [*to_slopes[: count + 1], to_slopes[count + 1 + m], pinned(slopes[m])],
                [shape((count * row_count, width_hidden), F32)],
                name="late",
                aliases={count + 2: 0},
            )[0]
    for m in batches:
        cotangent = cotangents[m]
        order = [mask for mask in masks if paired]
        sent = {mask: swapped(cotangent, "dp", mask) for mask in (order if m else reversed(order))}
        near = [cotangent] + [sent[mask] for mask in order]
        count = len(near)
        places = [[0, *range(3, count)], list(range(1, min(count, 3)))] if count > 1 else [[0]]
        made = [
            call(
                functools.partial(hidden_kernel, part),
                [
                    *[pinned(near[place]) for place in part],
                    scales, turned_out, pinned(slopes[m]) if paired else saved[m][3],
                ],
                [shape((len(part) * row_count, width_hidden))],
                [pltpu.VMEM((len(part) * row_count, width), BF16)],
                name="hidden",
                ordered=False,
            )[0]
            for part in places
        ]
        hidden_blocks += made
        if paired:
            crossed = [swapped(part, "dp", 1) for part in made]
            hidden_blocks += crossed
    if not paired:
        grad_rows = jnp.concatenate(hidden_blocks, axis=0)
        return (
            plain_square(merged, owner_table, owners, total_rows)[None],
            plain_square(grad_rows, owner_table, owners, total_rows)[None],
        )
    late = len(crossed)
    earlier, act_share = owned_partial(call, hidden_blocks[:-late], owned, owners, factor, [own, other])
    grad_share = owned_square(call, hidden_blocks[-late:], owned, owners, factor, earlier)
    return (act_share[None], grad_share[None])


def solution(mesh):
    placed = (
        P(None, "dp", None),
        P("section", None),
        P("section", None, None),
        P("section", None, None),
        P("section", None),
        P(None, "dp", None),
        P(),
    )
    return jax.shard_map(
        body,
        mesh=mesh,
        in_specs=placed,
        out_specs=(P("section", "dp", None), P("section", "dp", None)),
        check_vma=False,
    )
```
